32 devices in a mesh: dp: 16 (over z, y, x), blk: 2 (over core).
Axes of the slice: x: 2, y: 2, z: 4, core: 2. Of those that a mesh axis runs over, the one named last changes fastest.
Arguments:
- short_tokens: bfloat16 [16384, 768], P(('dp', 'blk')), may hold values from -6 to 6
- short_lengths: int32 [32, 16], P(('dp', 'blk')), may hold values from 1 to 64, 512 in all within a row
- long_tokens: bfloat16 [32, 512, 768], P('dp', 'blk'), may hold values from -6 to 6
- long_lengths: int32 [32], P('dp'), may hold values from 257 to 512, as said below
- eval_tokens: bfloat16 [16384, 768], P(('dp', 'blk')), may hold values from -6 to 6
- eval_lengths: int32 [32, 16], P(('dp', 'blk')), may hold values from 1 to 64, 512 in all within a row
- query_matrix: bfloat16 [768, 768], replicated, may hold values from -0.21875 to 0.21875
- key_weight: bfloat16 [768, 768], replicated, may hold values from -0.21875 to 0.21875
- value_matrix: bfloat16 [768, 768], replicated, may hold values from -0.21875 to 0.21875
- out_weight: bfloat16 [768, 768], replicated, may hold values from -0.875 to 0.875
- inner_weight: bfloat16 [768, 3072], replicated, may hold values from -0.21875 to 0.21875
- outer_weight: bfloat16 [3072, 768], replicated, may hold values from -0.109375 to 0.109375
- query_down_factor: bfloat16 [768, 8], replicated, may hold values from -0.21875 to 0.21875
- query_up_factor: bfloat16 [8, 768], replicated, may hold values from -1 to 1
- value_down_factor: bfloat16 [768, 8], replicated, may hold values from -0.21875 to 0.21875
- value_up_factor: bfloat16 [8, 768], replicated, may hold values from -1 to 1
- attention_gain: float32 [768], replicated, may hold values from 0.1 to 1.9
- output_gain: float32 [768], replicated, may hold values from 0.1 to 1.9
- cot_short: float32 [16384, 768], P(('dp', 'blk')), may hold values from -6 to 6
- cot_long: float32 [32, 512, 768], P('dp', 'blk'), may hold values from -6 to 6
Outputs:
- short_out: bfloat16 [16384, 768], P(('dp', 'blk'))
- long_out: bfloat16 [32, 512, 768], P('dp', 'blk')
- short_grad: float32 [16384, 768], P(('dp', 'blk'))
- long_grad: float32 [32, 512, 768], P('dp', 'blk')
- query_up_grad: float32 [8, 768], replicated
- value_up_grad: float32 [8, 768], replicated
- eval_out: bfloat16 [16384, 768], P(('dp', 'blk'))
The draws below stay inside these ranges and needn't reach their ends.
Inputs may be any that keep to these rules, and one draw needn't show every extreme that they name: `long_lengths`: the first long item has length 512 in every draw; every long item is longer than half of 512. `short_lengths`: each device's row of 16 lengths sums to 512; its largest is 64. `eval_lengths`: each device's row of 16 lengths sums to 512; its largest is 64.
All inputs are finite; a program needn't handle non-finite values.
Results may differ from the reference program's by a relative error of at most 0.013.
The reference program's roundings to bfloat16 on the way count: a program that leaves them out, or rounds other values in their place, can miss the bound.
Values may be sent and summed in bfloat16 or wider, within the bound.
No kernel may reach another device: no remote copies, remote signals or barrier semaphores. Data moves between devices by JAX's collectives and lax.ppermute only.
A program may use at most 192 MiB of HBM per device.

```python
import math
import jax
import jax.numpy as jnp
import numpy as np
from jax import lax

D = 768
HEADS = 12
HEAD = 64
FF = 3072
RANK = 8
SHORT_MOST = 64
LONG_LEN = 512
SHORT_DEV = 512
ITEMS_DEV = 16
SHORT_ROWS = 16384
LONG_ITEMS = 32
N_DP = 16
N_BLK = 2


def draw_long_lengths(key, part):
    key = jax.random.fold_in(key, 7)
    drawn = jax.random.randint(key, (LONG_ITEMS,), LONG_LEN // 2 + 1, LONG_LEN + 1, dtype=jnp.int32)
    return drawn.at[0].set(LONG_LEN).astype(jnp.int32)


def shard_levels(stream_key, dims, pieces, smallest, high):
    level, own = 1.0, jax.random.fold_in(stream_key, 6)
    for dim, blocks in pieces:
        heights = jnp.exp(jax.random.uniform(jax.random.fold_in(own, dim), (blocks,), jnp.float32, smallest / len(pieces), high / len(pieces)))
        level = level * jnp.repeat(heights, dims[dim] // blocks).reshape([-1 if axis == dim else 1 for axis in range(len(dims))])
    return level


def length_profile(count, total, limit, slope):
    portions = [(1 << 20) // math.isqrt(grade ** slope) + 1 for grade in range(2, count + 1)]
    rest, given = total - limit - (count - 1), [1] * (count - 1)
    while rest > 0:
        candidates = [i for i in range(count - 1) if given[i] < limit]
        whole, left = sum([portions[i] for i in candidates]), rest
        for i in candidates:
            addition = min(limit - given[i], max(1, left * portions[i] // whole), rest)
            given[i] = given[i] + addition
            rest = rest - addition
    return np.array([limit] + given)


def ragged_sizes(key, count, total, limit, skew):
    if count == 2:
        one = jax.random.randint(key, (), max(1, total - limit), min(limit, total - 1) + 1)
        return jnp.stack([one, total - one])
    lengths = jnp.asarray(length_profile(count, total, limit, skew), jnp.int32)
    couples = (count - 1) // 2
    giver, receiver = lengths[1:1 + 2 * couples:2], lengths[2:2 + 2 * couples:2]
    slack = jnp.minimum(giver - 1, limit - receiver)
    shifted = jax.random.randint(jax.random.fold_in(key, 1), (couples,), 0, 1 << 20) % (slack + 1)
    lengths = lengths.at[1:1 + 2 * couples:2].set(giver - shifted).at[2:2 + 2 * couples:2].set(receiver + shifted)
    return lengths[jax.random.permutation(jax.random.fold_in(key, 2), count)]


def normal_values(own_key, shape, spread, limit, split=(), kind=jnp.bfloat16):
    array = spread * jax.random.normal(own_key, shape, jnp.float32)
    if split:
        array = array * shard_levels(own_key, shape, split, -0.22, 0.18)
    return jnp.clip(array, -limit, limit).astype(kind)


def setup_inputs(seed: int = 0) -> dict:
    key_of = jax.random.split(jax.random.key(seed), 21)
    short_tokens = normal_values(key_of[0], (SHORT_ROWS, D), 1.0, 6.0, ((0, 32),))
    short_lengths = jax.vmap(lambda own: ragged_sizes(own, ITEMS_DEV, SHORT_DEV, SHORT_MOST, 2))(jax.random.split(key_of[1], (N_DP * N_BLK))).reshape((N_DP * N_BLK, ITEMS_DEV)).astype(jnp.int32)
    long_tokens = normal_values(key_of[2], (LONG_ITEMS, LONG_LEN, D), 1.0, 6.0, ((0, 16), (1, 2)))
    long_lengths = draw_long_lengths(jax.random.fold_in(key_of[20], 71), 0)
    eval_tokens = normal_values(key_of[4], (SHORT_ROWS, D), 1.0, 6.0, ((0, 32),))
    eval_lengths = jax.vmap(lambda own: ragged_sizes(own, ITEMS_DEV, SHORT_DEV, SHORT_MOST, 2))(jax.random.split(key_of[5], (N_DP * N_BLK))).reshape((N_DP * N_BLK, ITEMS_DEV)).astype(jnp.int32)
    query_matrix = normal_values(key_of[6], (D, D), D ** -0.5, 0.21875)
    key_weight = normal_values(key_of[7], (D, D), D ** -0.5, 0.21875)
    value_matrix = normal_values(key_of[8], (D, D), D ** -0.5, 0.21875)
    out_weight = normal_values(key_of[9], (D, D), (D // 16) ** -0.5, 0.875)
    inner_weight = normal_values(key_of[10], (D, FF), D ** -0.5, 0.21875)
    outer_weight = normal_values(key_of[11], (FF, D), FF ** -0.5, 0.109375)
    query_down_factor = normal_values(key_of[12], (D, RANK), D ** -0.5, 0.21875)
    query_up_factor = normal_values(key_of[13], (RANK, D), (4 * RANK) ** -0.5, 1.0)
    value_down_factor = normal_values(key_of[14], (D, RANK), D ** -0.5, 0.21875)
    value_up_factor = normal_values(key_of[15], (RANK, D), (4 * RANK) ** -0.5, 1.0)
    attention_gain = jnp.clip(1.0 + 0.18 * jax.random.normal(key_of[16], (D,), jnp.float32), 0.1, 1.9)
    output_gain = jnp.clip(1.0 + 0.18 * jax.random.normal(key_of[17], (D,), jnp.float32), 0.1, 1.9)
    cot_short = normal_values(key_of[18], (SHORT_ROWS, D), 1.0, 6.0, ((0, 32),), jnp.float32)
    cot_long = normal_values(key_of[19], (LONG_ITEMS, LONG_LEN, D), 1.0, 6.0, ((0, 16), (1, 2)), jnp.float32)
    return {"short_tokens": short_tokens, "short_lengths": short_lengths, "long_tokens": long_tokens, "long_lengths": long_lengths, "eval_tokens": eval_tokens, "eval_lengths": eval_lengths, "query_matrix": query_matrix, "key_weight": key_weight, "value_matrix": value_matrix, "out_weight": out_weight, "inner_weight": inner_weight, "outer_weight": outer_weight, "query_down_factor": query_down_factor, "query_up_factor": query_up_factor, "value_down_factor": value_down_factor, "value_up_factor": value_up_factor, "attention_gain": attention_gain, "output_gain": output_gain, "cot_short": cot_short, "cot_long": cot_long}


@jax.custom_vjp
def reduced_rank(v):
    return lax.optimization_barrier(v.astype(jnp.bfloat16)).astype(jnp.float32)

@jax.custom_vjp
def low_back(v):
    return v

def low_keep(v):
    return (reduced_rank(v), None)

def low_pass(kept, grad):
    return (grad,)

def back_keep(v):
    return (v, None)

def back_low(kept, grad):
    return (reduced_rank(grad),)
reduced_rank.defvjp(low_keep, low_pass)
low_back.defvjp(back_keep, back_low)
adapter_scale = 2.0
norm_eps = 1e-05
masked_score = -1000000000.0

def precise_product(left, right):
    return jnp.dot(left, right, precision=lax.Precision.HIGHEST)

def round_operands(value):
    return reduced_rank(low_back(value))

def normalize(value):
    centre = value - lax.optimization_barrier(jnp.mean(value, axis=-1, keepdims=True))
    return centre * lax.rsqrt(lax.optimization_barrier(jnp.mean(centre * centre, axis=-1, keepdims=True)) + norm_eps)

def segment_mask(row_lengths, rows):
    ends = jnp.cumsum(row_lengths.astype(jnp.int32))
    positions = jnp.arange(rows, dtype=jnp.int32)
    segment = lax.optimization_barrier(jnp.sum((positions[:, None] >= ends[None, :]).astype(jnp.int32), axis=1))
    return segment[:, None] == segment[None, :]

def layer_block(token_rows, key_mask, fixed_params, adapters):
    query_matrix, key_weight, value_matrix, out_weight, inner_weight, outer_weight, query_down_factor, value_down_factor, attention_gain, output_gain = fixed_params
    rows = token_rows.shape[0]
    if adapters is None:
        query_rows = round_operands(precise_product(token_rows, query_matrix))
        value_rows = round_operands(precise_product(token_rows, value_matrix))
    else:
        query_up_factor, value_up_factor = adapters
        query_reduced = round_operands(precise_product(token_rows, query_down_factor))
        value_reduced = round_operands(precise_product(token_rows, value_down_factor))
        query_rows = round_operands(precise_product(token_rows, query_matrix) + adapter_scale * precise_product(query_reduced, query_up_factor))
        value_rows = round_operands(precise_product(token_rows, value_matrix) + adapter_scale * precise_product(value_reduced, value_up_factor))
    key_rows = round_operands(precise_product(token_rows, key_weight))
    query_heads = query_rows.reshape(rows, HEADS, HEAD)
    key_heads = key_rows.reshape(rows, HEADS, HEAD)
    value_heads = value_rows.reshape(rows, HEADS, HEAD)
    raw_scores = jnp.einsum('qhd,khd->hqk', query_heads, key_heads, precision=lax.Precision.HIGHEST)
    scores = low_back(raw_scores * HEAD ** (-0.5))
    scores = jnp.where(key_mask[None], scores, masked_score)
    maxima = lax.optimization_barrier(jnp.max(scores, axis=-1, keepdims=True))
    powers = jnp.exp(scores - maxima)
    shares = reduced_rank(powers / lax.optimization_barrier(jnp.sum(powers, axis=-1, keepdims=True)))
    mixed = jnp.einsum('hqk,khd->qhd', shares, value_heads, precision=lax.Precision.HIGHEST)
    context = round_operands(mixed.reshape(rows, D))
    attended = low_back(precise_product(context, out_weight))
    first = token_rows + attended
    middle = normalize(first) * attention_gain
    inner = low_back(precise_product(reduced_rank(middle), inner_weight))
    hidden = reduced_rank(jax.nn.gelu(inner, approximate=False))
    outer = low_back(precise_product(hidden, outer_weight))
    return normalize(middle + outer) * output_gain

def reference(short_tokens, short_lengths, long_tokens, long_lengths, eval_tokens, eval_lengths, query_matrix, key_weight, value_matrix, out_weight, inner_weight, outer_weight, query_down_factor, query_up_factor, value_down_factor, value_up_factor, attention_gain, output_gain, cot_short, cot_long):
    fixed_params = tuple((weight.astype(jnp.float32) for weight in (query_matrix, key_weight, value_matrix, out_weight, inner_weight, outer_weight, query_down_factor, value_down_factor, attention_gain, output_gain)))

    def forward(short_in, long_in, query_adapter, value_adapter):
        adapters = (query_adapter, value_adapter)

        def short_item(pair):
            return layer_block(pair[0], segment_mask(pair[1], SHORT_DEV), fixed_params, adapters)

        def long_item(pair):
            visible = jnp.arange(LONG_LEN, dtype=jnp.int32) < pair[1]
            return layer_block(pair[0], jnp.broadcast_to(visible[None, :], (LONG_LEN, LONG_LEN)), fixed_params, adapters)
        short_result = lax.map(jax.checkpoint(short_item), (short_in.reshape(N_DP * N_BLK, SHORT_DEV, D), short_lengths))
        long_result = lax.map(jax.checkpoint(long_item), (long_in, long_lengths))
        return (short_result.reshape(SHORT_ROWS, D), long_result)
    outputs, pullback = jax.vjp(forward, short_tokens.astype(jnp.float32), long_tokens.astype(jnp.float32), query_up_factor.astype(jnp.float32), value_up_factor.astype(jnp.float32))
    short_grad, long_grad, query_up_grad, value_up_grad = pullback((cot_short, cot_long))
    combined_query_weight = reduced_rank(fixed_params[0] + adapter_scale * precise_product(fixed_params[6], query_up_factor.astype(jnp.float32)))
    combined_value_weight = reduced_rank(fixed_params[2] + adapter_scale * precise_product(fixed_params[7], value_up_factor.astype(jnp.float32)))
    eval_frozen = (combined_query_weight, fixed_params[1], combined_value_weight) + fixed_params[3:]

    def eval_item(pair):
        return layer_block(pair[0], segment_mask(pair[1], SHORT_DEV), eval_frozen, None)
    eval_out = lax.map(eval_item, (eval_tokens.astype(jnp.float32).reshape(N_DP * N_BLK, SHORT_DEV, D), eval_lengths)).reshape(SHORT_ROWS, D)
    return (outputs[0].astype(jnp.bfloat16), outputs[1].astype(jnp.bfloat16), short_grad, long_grad, query_up_grad, value_up_grad, eval_out.astype(jnp.bfloat16))
```

```python
import functools

import jax
import jax.numpy as jnp
from jax import lax
from jax.experimental import pallas as pl
from jax.experimental.pallas import tpu as pltpu
from jax.sharding import PartitionSpec as P

HEADS = 12
HEAD = 64
STACK = 4
WIDE = STACK * HEAD
GROUPS = HEADS // STACK
BLOCK = 128
WINDOW = 256
REACH = 64
LANES = 128
RANK = 8
VMEM_LIMIT = 56 * 2**20
CHUNK = 1024

adapter_scale = 2.0
norm_eps = 1e-05
masked_score = -1000000000.0
head_scale = HEAD ** (-0.5)

bf16 = jnp.bfloat16
f32 = jnp.float32


def nn(left, right):
    return jnp.dot(left, right, preferred_element_type=f32)


def nt(left, right):
    return lax.dot_general(left, right, (((1,), (1,)), ((), ())), preferred_element_type=f32)


def tn(left, right):
    return lax.dot_general(left, right, (((0,), (0,)), ((), ())), preferred_element_type=f32)


def fill_factors(query_down, value_down, query_up, value_up, down, query_rows, value_rows):
    width = down.shape[1]
    blank = jnp.zeros((RANK, width), f32)
    rest = jnp.zeros((LANES - 2 * RANK, width), bf16)
    query_two = adapter_scale * query_up[...].astype(f32)
    value_two = adapter_scale * value_up[...].astype(f32)
    both = [query_down[...].astype(f32), value_down[...].astype(f32)]
    for target, parts in (
        (down, both), (query_rows, [query_two, blank]), (value_rows, [blank, value_two]),
    ):
        target[0 : 2 * RANK, :] = jnp.concatenate(parts, axis=0).astype(bf16)
        target[2 * RANK :, :] = rest


def head_masks():
    lane = lax.broadcasted_iota(jnp.int32, (1, WIDE), 1)
    return [(lane >= h * HEAD) & (lane < (h + 1) * HEAD) for h in range(STACK)]


def stack_heads(value):
    zero = jnp.zeros_like(value)
    return jnp.concatenate([jnp.where(mask, value, zero) for mask in head_masks()], axis=0)


def unstack_heads(value):
    rows = value.shape[0] // STACK
    lane = lax.broadcasted_iota(jnp.int32, (1, LANES), 1)
    low = lane < HEAD
    parts = []
    for pair in range(STACK // 2):
        columns = slice(pair * LANES, (pair + 1) * LANES)
        first = value[2 * pair * rows : (2 * pair + 1) * rows, columns]
        second = value[(2 * pair + 1) * rows : (2 * pair + 2) * rows, columns]
        parts.append(jnp.where(low, first, second))
    return jnp.concatenate(parts, axis=1)


def normalize(value):
    centre = value - jnp.mean(value, axis=-1, keepdims=True)
    inverse = lax.rsqrt(jnp.mean(centre * centre, axis=-1, keepdims=True) + norm_eps)
    return centre * inverse, inverse


def normalize_back(grad, unit, inverse):
    return inverse * (
        grad
        - jnp.mean(grad, axis=-1, keepdims=True)
        - unit * jnp.mean(grad * unit, axis=-1, keepdims=True)
    )


def segment_bias(lengths, bias, rows):
    key_place = lax.broadcasted_iota(jnp.int32, (rows, LANES), 0)
    query_place = lax.broadcasted_iota(jnp.int32, (8, rows), 1)
    key_segment = jnp.zeros((rows, LANES), jnp.int32)
    query_segment = jnp.zeros((8, rows), jnp.int32)
    end = jnp.int32(0)
    for item in range(lengths.shape[1]):
        end = end + lengths[0, item]
        key_segment = key_segment + (key_place >= end).astype(jnp.int32)
        query_segment = query_segment + (query_place >= end).astype(jnp.int32)
    for block in range(rows // BLOCK):
        start = window_start(block, rows)
        same = (
            key_segment[start : start + WINDOW, :]
            == query_segment[0:1, block * BLOCK : (block + 1) * BLOCK]
        )
        bias[block] = jnp.where(same, 0.0, masked_score)


def window_start(block, rows):
    return min(max(block * BLOCK - REACH, 0), rows - WINDOW)


def run_tasks(tasks):
    rest = None
    for products, after in tasks:
        value = products()
        if rest is not None:
            rest()
        rest = functools.partial(after, value)
    rest()


def softmax_columns(scores):
    peak = jnp.max(scores, axis=0, keepdims=True)
    powers = jnp.exp(scores - peak)
    return powers * (1.0 / jnp.sum(powers, axis=0, keepdims=True))


def short_units(rows):
    for index in range(GROUPS):
        for block in range(rows // BLOCK):
            start = window_start(block, rows)
            yield (
                index, block, slice(index * WIDE, (index + 1) * WIDE),
                slice(block * BLOCK, (block + 1) * BLOCK), slice(start, start + WINDOW),
            )


def short_attention(queries, keys, values, bias, context, shares, rows):
    def task(index, block, columns, own, window):
        def products():
            return nt(keys[window, columns], stack_heads(queries[own, columns]))

        def rest(scores):
            exact = softmax_columns(scores + jnp.concatenate([bias[block]] * STACK, axis=1))
            if shares is not None:
                shares[index, block] = exact
            mixed = tn(exact.astype(bf16), values[window, columns])
            context[own, columns] = unstack_heads(mixed).astype(bf16)

        return products, rest

    run_tasks([task(*unit) for unit in short_units(rows)])


def short_attention_back(queries, keys, values, dcontext, shares, dqueries, dkeys, dvalues, rows):
    dkeys[...] = jnp.zeros_like(dkeys)
    dvalues[...] = jnp.zeros_like(dvalues)

    def task(index, block, columns, own, window):
        def products():
            dstacked = stack_heads(dcontext[own, columns])
            return dstacked, nt(values[window, columns], dstacked)

        def rest(value):
            dstacked, dshares = value
            exact = shares[index, block]
            inner = jnp.sum(exact * dshares, axis=0, keepdims=True)
            dscores = (exact * (dshares - inner)).astype(bf16)
            mixed = tn(dscores, keys[window, columns])
            dqueries[own, columns] = (unstack_heads(mixed) * head_scale).astype(bf16)
            dkeys[window, columns] += nn(dscores, stack_heads(queries[own, columns]))
            dvalues[window, columns] += nn(exact.astype(bf16), dstacked)

        return products, rest

    run_tasks([task(*unit) for unit in short_units(rows)])


def project_to(tokens, low, weight, extra, scale=None):
    value = nn(tokens, weight)
    if extra is not None:
        value = value + nn(low, extra)
    value = value.astype(bf16)
    return value if scale is None else value * jnp.asarray(scale, bf16)


def dense_tasks(tokens, context, weights, gains, hidden, out, kept=None, ready=None):
    out_weight, inner_weight, outer_weight = weights
    attention_gain, output_gain = gains
    rows, width = tokens.shape
    halves = [slice(0, rows // 2), slice(rows // 2, rows)]
    chunks = [slice(start, start + CHUNK) for start in range(0, hidden.shape[1], CHUNK)]
    ready = ready or {}
    unit, inverse = (kept["unit"], kept["inverse"]) if kept else (ready["unit"], None)
    low = out

    def wait(name):
        if name in ready:
            ready.pop(name)()

    def attend_out(r):
        def products():
            wait("out")
            return nn(context[r, :], out_weight[...])

        def rest(value):
            scaled, factor = normalize(tokens[r, :].astype(f32) + value)
            if kept:
                inverse[r, :] = factor
                unit[r, :] = scaled
                low[r, :] = (scaled * attention_gain).astype(bf16)
            else:
                middle = scaled * attention_gain
                unit[r, :] = middle
                low[r, :] = middle.astype(bf16)

        return products, rest

    def inner_part(r, columns):
        def products():
            wait(("inner", columns.start))
            return nn(low[r, :], inner_weight[:, columns])

        def rest(inner):
            phi = 0.5 + 0.5 * lax.erf(inner * 0.7071067811865476)
            hidden[r, columns] = (inner * phi).astype(bf16)
            if kept:
                kept["slope"][r, columns] = phi + inner * (
                    jnp.exp(-0.5 * inner * inner) * 0.3989422804014327
                )

        return products, rest

    def outer_part(r):
        def products():
            wait("outer")
            return nn(hidden[r, :], outer_weight[...])

        def rest(value):
            middle = unit[r, :] * attention_gain if kept else unit[r, :]
            scaled, factor = normalize(middle + value)
            out[r, :] = (scaled * output_gain).astype(bf16)
            if kept:
                dsecond = normalize_back(kept["cotangent"][r, :] * output_gain, scaled, factor)
                kept["dfirst"][r, :] = dsecond
                kept["dlow"][r, :] = dsecond.astype(bf16)

        return products, rest

    def outer_back(r, columns):
        def products():
            return nt(kept["dlow"][r, :], outer_weight[columns, :])

        def rest(dhidden):
            hidden[r, columns] = (dhidden * kept["slope"][r, columns]).astype(bf16)

        return products, rest

    def inner_back(r):
        def products():
            return nt(hidden[r, :], inner_weight[...])

        def rest(value):
            dmiddle = kept["dfirst"][r, :] + value
            dfirst = normalize_back(dmiddle * attention_gain, unit[r, :], inverse[r, :])
            kept["dfirst"][r, :] = dfirst
            kept["dlow"][r, :] = dfirst.astype(bf16)

        return products, rest

    def attend_back(r):
        def products():
            return nt(kept["dlow"][r, :], out_weight[...])

        def rest(value):
            kept["dcontext"][r, :] = value.astype(bf16)

        return products, rest

    tasks = [attend_out(r) for r in halves]
    tasks += [inner_part(r, columns) for r in halves for columns in chunks]
    tasks += [outer_part(r) for r in halves]
    if kept:
        tasks += [outer_back(r, columns) for r in halves for columns in chunks]
        tasks += [inner_back(r) for r in halves]
        tasks += [attend_back(r) for r in halves]
    return tasks


class Copies:
    def __init__(self, semaphores):
        self.semaphores = semaphores
        self.count = 0

    def start(self, source, target):
        copy = pltpu.make_async_copy(source, target, self.semaphores.at[self.count])
        self.count += 1
        copy.start()
        return copy


def start_all(copies, pairs):
    return [copies.start(source, target) for source, target in pairs]


def short_kernel(
    lengths, query_down, query_up, value_down, value_up, attention_gain_in, output_gain_in,
    tokens_in, cotangent_in, query_in, key_in, value_in, out_in, inner_in, outer_in,
    out_out, grad_out, up_out,
    tokens, cotangent, query_weight, key_weight, value_weight, out_weight, inner_weight, outer_weight,
    down, query_rows, value_rows, bias, queries, keys, values, context, shares,
    unit, inverse, dfirst, slope, hidden, out, dlow, semaphores,
):
    rows, width = tokens.shape
    copies = Copies(semaphores)
    waits = start_all(
        copies,
        (
            (tokens_in, tokens), (query_in, query_weight), (key_in, key_weight), (value_in, value_weight),
            (out_in, out_weight), (inner_in, inner_weight), (outer_in, outer_weight),
            (cotangent_in, cotangent),
        ),
    )
    fill_factors(query_down, value_down, query_up, value_up, down, query_rows, value_rows)
    segment_bias(lengths, bias, rows)
    gains = (attention_gain_in[...].reshape(1, width), output_gain_in[...].reshape(1, width))
    waits[0].wait()
    low = nt(tokens[...], down[...]).astype(bf16)
    waits[1].wait()
    queries[...] = project_to(tokens[...], low, query_weight[...], query_rows[...], head_scale)
    waits[2].wait()
    keys[...] = project_to(tokens[...], low, key_weight[...], None)
    waits[3].wait()
    values[...] = project_to(tokens[...], low, value_weight[...], value_rows[...])
    short_attention(queries, keys, values, bias, context, shares, rows)
    for wait in waits[4:]:
        wait.wait()
    dense = (out_weight, inner_weight, outer_weight)
    dcontext = context
    kept = dict(
        unit=unit, inverse=inverse, dfirst=dfirst, slope=slope, dlow=dlow, cotangent=cotangent, dcontext=dcontext,
    )
    run_tasks(dense_tasks(tokens, context, dense, gains, hidden, out, kept))
    sent = [copies.start(out, out_out)]
    dqueries = hidden.at[:, 0:width]
    dkeys, dvalues = slope.at[:, 0:width], slope.at[:, width : 2 * width]
    short_attention_back(queries, keys, values, dcontext, shares, dqueries, dkeys, dvalues, rows)
    dquery = dqueries[...]
    dkey = dkeys[...].astype(bf16)
    dvalue = dvalues[...].astype(bf16)
    low = nt(tokens[...], down[...]).astype(bf16)
    dlatent = (nt(dquery, query_rows[...]) + nt(dvalue, value_rows[...])).astype(bf16)
    cotangent[...] = (
        dfirst[...]
        + nt(dquery, query_weight[...])
        + nt(dkey, key_weight[...])
        + nt(dvalue, value_weight[...])
        + nn(dlatent, down[...])
    )
    sent.append(copies.start(cotangent, grad_out))
    up_out[0:RANK, :] = adapter_scale * tn(low, dquery)[0:RANK, :]
    up_out[RANK : 2 * RANK, :] = adapter_scale * tn(low, dvalue)[RANK : 2 * RANK, :]
    for copy in sent:
        copy.wait()


def long_kernel(
    lengths, query_down, query_up, value_down, value_up, attention_gain_in, output_gain_in, short_up,
    tokens_in, far_in, cotangent_in, query_in, key_in, value_in, out_in, inner_in, outer_in,
    out_out, near_out, far_out, up_out,
    tokens, far, cotangent, query_weight, key_weight, value_weight, out_weight, inner_weight, outer_weight,
    down, query_rows, value_rows, queries, keys, values, context, shares,
    unit, inverse, dfirst, slope, hidden, out, dlow, low, semaphores,
):
    rows, width = tokens.shape
    items = lengths.shape[0]
    half = rows // items
    copies = Copies(semaphores)
    waits = start_all(
        copies,
        (
            (tokens_in, tokens), (query_in, query_weight), (far_in, far), (key_in, key_weight),
            (value_in, value_weight), (out_in, out_weight), (inner_in, inner_weight), (outer_in, outer_weight),
            (cotangent_in, cotangent),
        ),
    )
    fill_factors(query_down, value_down, query_up, value_up, down, query_rows, value_rows)
    gains = (attention_gain_in[...].reshape(1, width), output_gain_in[...].reshape(1, width))
    place = lax.axis_index("blk")

    def part(item, which):
        start = 2 * item * half + (place if which == 0 else 1 - place) * half
        return pl.ds(pl.multiple_of(start, half), half)

    def put(target, which, value):
        for item in range(items):
            target[part(item, which), :] = value[item * half : (item + 1) * half]

    waits[0].wait()
    low[0:rows, :] = nt(tokens[...], down[...]).astype(bf16)
    waits[1].wait()
    queries[...] = project_to(tokens[...], low[0:rows, :], query_weight[...], query_rows[...], head_scale)
    waits[2].wait()
    low[rows:, :] = nt(far[...], down[...]).astype(bf16)
    waits[3].wait()
    put(keys, 0, project_to(tokens[...], None, key_weight[...], None))
    put(keys, 1, project_to(far[...], None, key_weight[...], None))
    waits[4].wait()
    put(values, 0, project_to(tokens[...], low[0:rows, :], value_weight[...], value_rows[...]))
    put(values, 1, project_to(far[...], low[rows:, :], value_weight[...], value_rows[...]))

    units = [
        (
            item * GROUPS + index, item, slice(index * WIDE, (index + 1) * WIDE),
            slice(item * half, (item + 1) * half), slice(2 * item * half, 2 * (item + 1) * half),
        )
        for item in range(items)
        for index in range(GROUPS)
    ]
    place_in_half = lax.broadcasted_iota(jnp.int32, (half, LANES), 0) + half
    masks = []
    for item in range(items):
        mask = jnp.where(place_in_half < lengths[item], 0.0, masked_score)
        masks.append(jnp.concatenate([mask] * (half // LANES), axis=1))

    def forward(number, item, columns, own, joined):
        state = {}

        def task(h):
            head = slice(h * half, (h + 1) * half)

            def products():
                if h == 0:
                    state["queries"] = stack_heads(queries[own, columns])
                    state["values"] = jnp.swapaxes(values[joined, columns], 0, 1)
                    state["context"] = []
                return nt(keys[joined, columns], state["queries"][head])

            def rest(scores):
                scores = jnp.concatenate([scores[0:half], scores[half:] + masks[item]], axis=0)
                exact = softmax_columns(scores).astype(bf16)
                shares[number, :, head] = exact
                state["context"].append(nn(state["values"][h * HEAD : (h + 1) * HEAD], exact))
                if h == STACK - 1:
                    mixed = jnp.concatenate(state["context"], axis=0)
                    context[own, columns] = jnp.swapaxes(mixed, 0, 1).astype(bf16)

            return products, rest

        return [task(h) for h in range(STACK)]

    run_tasks([task for unit_ in units for task in forward(*unit_)])
    for wait in waits[5:]:
        wait.wait()
    dense = (out_weight, inner_weight, outer_weight)
    dcontext = context
    kept = dict(
        unit=unit, inverse=inverse, dfirst=dfirst, slope=slope, dlow=dlow, cotangent=cotangent, dcontext=dcontext,
    )
    run_tasks(dense_tasks(tokens, context, dense, gains, hidden, out, kept))
    sent = [copies.start(out, out_out)]
    dqueries = dlow
    dkeys = hidden.at[:, 0 : 2 * width]
    dvalues = hidden.at[:, 2 * width : 4 * width]

    def backward(number, item, columns, own, joined):
        state = {}

        def task(h):
            head = slice(h * half, (h + 1) * half)

            def products():
                if h == 0:
                    state["dcontext"] = stack_heads(dcontext[own, columns])
                    state["keys"] = jnp.swapaxes(keys[joined, columns], 0, 1)
                    state["dscores"], state["dqueries"] = [], []
                return nt(values[joined, columns], state["dcontext"][head])

            def rest(dshares):
                exact = shares[number, :, head].astype(f32)
                inner = jnp.sum(exact * dshares, axis=0, keepdims=True)
                dscores = (exact * (dshares - inner)).astype(bf16)
                state["dscores"].append(dscores)
                state["dqueries"].append(nn(state["keys"][h * HEAD : (h + 1) * HEAD], dscores))
                if h == STACK - 1:
                    mixed = jnp.concatenate(state["dqueries"], axis=0) * head_scale
                    dqueries[own, columns] = jnp.swapaxes(mixed, 0, 1).astype(bf16)
                    stacked = stack_heads(queries[own, columns])
                    dkey = nn(jnp.concatenate(state["dscores"], axis=1), stacked).astype(bf16)
                    dvalue = nn(shares[number], state["dcontext"]).astype(bf16)
                    for which in range(2):
                        rows_ = slice(which * half, (which + 1) * half)
                        target = slice(which * width + columns.start, which * width + columns.stop)
                        dkeys[own, target] = dkey[rows_]
                        dvalues[own, target] = dvalue[rows_]

            return products, rest

        return [task(h) for h in range(STACK)]

    run_tasks([task for unit_ in units for task in backward(*unit_)])

    def back_part(which):
        start = pl.multiple_of((place if which == 0 else 1 - place) * width, LANES)
        return dkeys[:, pl.ds(start, width)], dvalues[:, pl.ds(start, width)]

    dkey, dvalue = back_part(1)
    dlatent = nt(dvalue, value_rows[...]).astype(bf16)
    unit[...] = nt(dkey, key_weight[...]) + nt(dvalue, value_weight[...]) + nn(dlatent, down[...])
    sent.append(copies.start(unit, far_out))
    up = tn(low[rows:, :], dvalue)[RANK : 2 * RANK, :]
    dquery = dqueries[...]
    dkey, dvalue = back_part(0)
    dlatent = (nt(dquery, query_rows[...]) + nt(dvalue, value_rows[...])).astype(bf16)
    cotangent[...] = (
        dfirst[...]
        + nt(dquery, query_weight[...])
        + nt(dkey, key_weight[...])
        + nt(dvalue, value_weight[...])
        + nn(dlatent, down[...])
    )
    sent.append(copies.start(cotangent, near_out))
    up = up + tn(low[0:rows, :], dvalue)[RANK : 2 * RANK, :]
    up_out[0:RANK, :] = adapter_scale * tn(low[0:rows, :], dquery)[0:RANK, :] + short_up[0:RANK, :]
    up_out[RANK : 2 * RANK, :] = adapter_scale * up + short_up[RANK : 2 * RANK, :]
    for copy in sent:
        copy.wait()


def eval_attention_kernel(
    lengths, query_down, query_up, value_down, value_up, after,
    tokens_in, query_in, key_in, value_in,
    context,
    tokens, query_weight, key_weight, value_weight,
    down, query_rows, value_rows, bias, queries, keys, values, semaphores,
):
    rows, width = tokens.shape
    copies = Copies(semaphores)
    waits = start_all(
        copies,
        (
            (tokens_in, tokens), (key_in, key_weight), (query_in, query_weight), (value_in, value_weight),
        ),
    )
    fill_factors(query_down, value_down, query_up, value_up, down, query_rows, value_rows)
    segment_bias(lengths, bias, rows)
    waits[0].wait()
    waits[1].wait()
    keys[...] = project_to(tokens[...], None, key_weight[...], None)
    waits[2].wait()
    merged = (query_weight[...].astype(f32) + tn(down[...], query_rows[...])).astype(bf16)
    queries[...] = project_to(tokens[...], None, merged, None, head_scale)
    waits[3].wait()
    merged = (value_weight[...].astype(f32) + tn(down[...], value_rows[...])).astype(bf16)
    values[...] = project_to(tokens[...], None, merged, None)
    short_attention(queries, keys, values, bias, context, None, rows)


def eval_dense_kernel(
    attention_gain_in, output_gain_in, after,
    tokens_in, context_in, out_in, inner_in, outer_in, near_in, far_in,
    out_out, grad_out,
    tokens, context, out_weight, inner_weight, outer_weight, near, far, unit, hidden, semaphores,
):
    width = tokens.shape[1]
    copies = Copies(semaphores)
    first = start_all(copies, ((context_in, context), (out_in, out_weight), (tokens_in, tokens)))
    inner = {}
    for start in range(0, hidden.shape[1], CHUNK):
        columns = slice(start, start + CHUNK)
        inner[start] = copies.start(inner_in.at[:, columns], inner_weight.at[:, columns])
    outer, *last = start_all(copies, ((outer_in, outer_weight), (near_in, near), (far_in, far)))
    gains = (attention_gain_in[...].reshape(1, width), output_gain_in[...].reshape(1, width))
    ready = {("inner", start): copy.wait for start, copy in inner.items()}
    ready["outer"] = outer.wait
    ready["unit"] = unit
    for wait in first:
        wait.wait()
    dense = (out_weight, inner_weight, outer_weight)
    run_tasks(dense_tasks(tokens, context, dense, gains, hidden, out_out, None, ready))
    for wait in last:
        wait.wait()
    near[...] = near[...] + far[...]
    copies.start(near, grad_out).wait()


IN_VMEM = pl.BlockSpec(memory_space=pltpu.VMEM)
IN_SMEM = pl.BlockSpec(memory_space=pltpu.SMEM)
ANYWHERE = pl.BlockSpec(memory_space=pl.ANY)
FACTORS = [IN_VMEM] * 4


def kernel_call(kernel, in_specs, out_specs, out_shape, scratch, copies, flops, moved, name):
    return pl.pallas_call(
        kernel,
        in_specs=in_specs,
        out_specs=out_specs,
        out_shape=out_shape,
        scratch_shapes=[*scratch, pltpu.SemaphoreType.DMA((copies,))],
        compiler_params=pltpu.CompilerParams(vmem_limit_bytes=VMEM_LIMIT),
        cost_estimate=pl.CostEstimate(flops=int(flops), bytes_accessed=int(moved), transcendentals=0),
        name=name,
    )


def shape(dims, kind):
    return jax.ShapeDtypeStruct(dims, kind)


def vm(dims, kind):
    return pltpu.VMEM(dims, kind)


def weight_room(width, wide):
    square = vm((width, width), bf16)
    return [square, square, square, square, vm((width, wide), bf16), vm((wide, width), bf16)]


def factor_room(width):
    return [vm((LANES, width), bf16)] * 3


def kept_room(rows, width, wide):
    return [
        vm((rows, width), f32), vm((rows, 1), f32), vm((rows, width), f32),
        vm((rows, wide), f32), vm((rows, wide), bf16), vm((rows, width), bf16), vm((rows, width), bf16),
    ]


def partner(value, axis, mask):
    count = lax.axis_size(axis)
    return lax.ppermute(value, axis, [(i, i ^ mask) for i in range(count)])


def quad_parts(value, axis, bit):
    masks = [mask * bit for mask in (1, 2, 3) if mask * bit < lax.axis_size(axis)]
    return [value, *[partner(value, axis, mask) for mask in masks]]


def add_up(parts):
    return functools.reduce(lambda a, b: a + b, parts)


def run_short(lengths, factors, gains, tokens, cotangent, weights):
    rows, width = tokens.shape
    wide = weights[4].shape[1]
    blocks = rows // BLOCK
    return kernel_call(
        short_kernel,
        [IN_SMEM, *FACTORS, IN_VMEM, IN_VMEM, *[ANYWHERE] * 8],
        [ANYWHERE, ANYWHERE, IN_VMEM],
        [shape((rows, width), bf16), shape((rows, width), f32), shape((2 * RANK, width), f32)],
        [
            vm((rows, width), bf16), vm((rows, width), f32), *weight_room(width, wide), *factor_room(width),
            vm((blocks, WINDOW, BLOCK), f32), *[vm((rows, width), bf16)] * 4,
            vm((GROUPS, blocks, WINDOW, STACK * BLOCK), f32), *kept_room(rows, width, wide),
        ],
        10, 20e9, 25e6, "short_step",
    )(lengths, *factors, *gains, tokens, cotangent, *weights)


def run_long(lengths, factors, gains, short_up, tokens, far, cotangent, weights):
    rows, width = tokens.shape
    wide = weights[4].shape[1]
    items = lengths.shape[0]
    half = rows // items
    return kernel_call(
        long_kernel,
        [IN_SMEM, *FACTORS, *[IN_VMEM] * 3, *[ANYWHERE] * 9],
        [ANYWHERE, ANYWHERE, ANYWHERE, IN_VMEM],
        [
            shape((rows, width), bf16), shape((rows, width), f32), shape((rows, width), f32),
            shape((2 * RANK, width), f32),
        ],
        [
            vm((rows, width), bf16), vm((rows, width), bf16), vm((rows, width), f32),
            *weight_room(width, wide), *factor_room(width), vm((rows, width), bf16),
            *[vm((2 * rows, width), bf16)] * 2, vm((rows, width), bf16),
            vm((items * GROUPS, 2 * half, STACK * half), bf16), *kept_room(rows, width, wide),
            vm((2 * rows, LANES), bf16),
        ],
        12, 22e9, 30e6, "long_step",
    )(lengths, *factors, *gains, short_up, tokens, far, cotangent, *weights)


def run_eval_attention(lengths, factors, after, tokens, weights):
    rows, width = tokens.shape
    blocks = rows // BLOCK
    return kernel_call(
        eval_attention_kernel,
        [IN_SMEM, *FACTORS, *[ANYWHERE] * 5],
        IN_VMEM,
        shape((rows, width), bf16),
        [
            vm((rows, width), bf16), *[vm((width, width), bf16)] * 3, *factor_room(width),
            vm((blocks, WINDOW, BLOCK), f32), *[vm((rows, width), bf16)] * 3,
        ],
        4, 4e9, 6e6, "eval_attention",
    )(lengths, *factors, after, tokens, *weights[0:3])


def run_eval_dense(gains, after, tokens, context, weights, near, far):
    rows, width = tokens.shape
    wide = weights[4].shape[1]
    return kernel_call(
        eval_dense_kernel,
        [IN_VMEM, IN_VMEM, *[ANYWHERE] * 8],
        [IN_VMEM, ANYWHERE],
        [shape((rows, width), bf16), shape((rows, width), f32)],
        [
            vm((rows, width), bf16), vm((rows, width), bf16), *weight_room(width, wide)[3:],
            vm((rows, width), f32), vm((rows, width), f32), vm((rows, width), f32), vm((rows, wide), bf16),
        ],
        12, 6e9, 18e6, "eval_dense",
    )(*gains, after, tokens, context, *weights[3:], near, far)


def body(
    short_tokens, short_lengths, long_tokens, long_lengths, eval_tokens, eval_lengths,
    query_matrix, key_weight, value_matrix, out_weight, inner_weight, outer_weight,
    query_down_factor, query_up_factor, value_down_factor, value_up_factor,
    attention_gain, output_gain, cot_short, cot_long,
):
    items, half, width = long_tokens.shape
    factors = (query_down_factor.T, query_up_factor, value_down_factor.T, value_up_factor)
    gains = (attention_gain, output_gain)
    weights = (query_matrix, key_weight, value_matrix, out_weight, inner_weight, outer_weight)

    long_flat = long_tokens.reshape(items * half, width)
    far_flat = partner(long_flat, "blk", 1)
    short_out, short_grad, short_up = run_short(
        short_lengths, factors, gains, short_tokens, cot_short, weights
    )
    long_out, near_grad, far_grad, up = run_long(
        long_lengths, factors, gains, short_up, long_flat, far_flat,
        cot_long.reshape(items * half, width), weights,
    )
    up = up + partner(up, "blk", 1)
    up, far_grad = lax.optimization_barrier((up, far_grad))
    arrived = partner(far_grad, "blk", 1)

    stages = []
    bit = 1
    while bit < lax.axis_size("dp"):
        stages.append(bit)
        bit *= 4
    parts = quad_parts(up, "dp", stages[0])
    context = run_eval_attention(eval_lengths, factors, up, eval_tokens, weights)
    context, *parts = lax.optimization_barrier((context, *parts))
    first_sum = add_up(parts)
    for bit in stages[1:]:
        parts = quad_parts(add_up(parts), "dp", bit)
    eval_out, long_grad = run_eval_dense(
        gains, first_sum, eval_tokens, context, weights, near_grad, arrived
    )
    eval_out, *parts = lax.optimization_barrier((eval_out, *parts))
    later_sum = add_up(parts)

    return (
        short_out,
        long_out.reshape(items, half, width),
        short_grad,
        long_grad.reshape(items, half, width),
        later_sum[0:RANK],
        later_sum[RANK:],
        eval_out,
    )


def solution(mesh):
    rows = P(("dp", "blk"), None)
    items = P("dp", "blk", None)
    return jax.shard_map(
        body,
        mesh=mesh,
        in_specs=(
            rows, rows, items, P("dp"), rows, rows, *[P()] * 12, rows, items,
        ),
        out_specs=(rows, items, rows, items, P(), P(), rows),
        check_vma=False,
    )
```

```python
import functools

import jax
import jax.numpy as jnp
from jax import lax
from jax.experimental import pallas as pl
from jax.experimental.pallas import tpu as pltpu
from jax.sharding import PartitionSpec as P

HEADS = 12
HEAD = 64
STACK = 4
WIDE = STACK * HEAD
GROUPS = HEADS // STACK
BLOCK = 128
WINDOW = 256
REACH = 64
LANES = 128
RANK = 8
VMEM_LIMIT = 62 * 2**20
CHUNK = 1024

adapter_scale = 2.0
norm_eps = 1e-05
masked_score = -1000000000.0
head_scale = HEAD ** (-0.5)

bf16 = jnp.bfloat16
f32 = jnp.float32


def nn(left, right):
    return jnp.dot(left, right, preferred_element_type=f32)


def nt(left, right):
    return lax.dot_general(left, right, (((1,), (1,)), ((), ())), preferred_element_type=f32)


def tn(left, right):
    return lax.dot_general(left, right, (((0,), (0,)), ((), ())), preferred_element_type=f32)


def fill_factors(query_down, value_down, query_up, value_up, down, query_rows, value_rows):
    width = down.shape[1]
    blank = jnp.zeros((RANK, width), f32)
    rest = jnp.zeros((LANES - 2 * RANK, width), bf16)
    query_two = adapter_scale * query_up[...].astype(f32)
    value_two = adapter_scale * value_up[...].astype(f32)
    both = [query_down[...].astype(f32), value_down[...].astype(f32)]
    for target, parts in (
        (down, both), (query_rows, [query_two, blank]), (value_rows, [blank, value_two]),
    ):
        target[0 : 2 * RANK, :] = jnp.concatenate(parts, axis=0).astype(bf16)
        target[2 * RANK :, :] = rest


def factor_pairs(factors, rooms):
    size = 2 * RANK
    return [
        (factors.at[i * size : (i + 1) * size, :], room.at[0:size, :]) for i, room in enumerate(rooms)
    ]


def clear_tails(rooms):
    for room in rooms:
        room[2 * RANK :, :] = jnp.zeros((LANES - 2 * RANK, room.shape[1]), bf16)


def head_masks():
    lane = lax.broadcasted_iota(jnp.int32, (1, WIDE), 1)
    return [(lane >= h * HEAD) & (lane < (h + 1) * HEAD) for h in range(STACK)]


def stack_heads(value):
    zero = jnp.zeros_like(value)
    return jnp.concatenate([jnp.where(mask, value, zero) for mask in head_masks()], axis=0)


def unstack_heads(value):
    rows = value.shape[0] // STACK
    lane = lax.broadcasted_iota(jnp.int32, (1, LANES), 1)
    low = lane < HEAD
    parts = []
    for pair in range(STACK // 2):
        columns = slice(pair * LANES, (pair + 1) * LANES)
        first = value[2 * pair * rows : (2 * pair + 1) * rows, columns]
        second = value[(2 * pair + 1) * rows : (2 * pair + 2) * rows, columns]
        parts.append(jnp.where(low, first, second))
    return jnp.concatenate(parts, axis=1)


def join_heads(turned, right, count):
    parts = [
        nn(turned[h * HEAD : (h + 1) * HEAD], right[:, h * count : (h + 1) * count]) for h in range(STACK)
    ]
    return jnp.swapaxes(jnp.concatenate(parts, axis=0), 0, 1)


def normalize(value):
    centre = value - jnp.mean(value, axis=-1, keepdims=True)
    inverse = lax.rsqrt(jnp.mean(centre * centre, axis=-1, keepdims=True) + norm_eps)
    return centre * inverse, inverse


def normalize_back(grad, unit, inverse):
    return inverse * (
        grad
        - jnp.mean(grad, axis=-1, keepdims=True)
        - unit * jnp.mean(grad * unit, axis=-1, keepdims=True)
    )


def segment_bias(lengths, bias, rows):
    key_place = lax.broadcasted_iota(jnp.int32, (rows, LANES), 0)
    query_place = lax.broadcasted_iota(jnp.int32, (8, rows), 1)
    key_segment = jnp.zeros((rows, LANES), jnp.int32)
    query_segment = jnp.zeros((8, rows), jnp.int32)
    end = jnp.int32(0)
    for item in range(lengths.shape[1]):
        end = end + lengths[0, item]
        key_segment = key_segment + (key_place >= end).astype(jnp.int32)
        query_segment = query_segment + (query_place >= end).astype(jnp.int32)
    for block in range(rows // BLOCK):
        start = window_start(block, rows)
        same = (
            key_segment[start : start + WINDOW, :]
            == query_segment[0:1, block * BLOCK : (block + 1) * BLOCK]
        )
        bias[block] = jnp.where(same, 0.0, masked_score)


def window_start(block, rows):
    return min(max(block * BLOCK - REACH, 0), rows - WINDOW)


def run_tasks(tasks):
    rest = None
    for products, after in tasks:
        value = products()
        if rest is not None:
            rest()
        rest = functools.partial(after, value)
    rest()


def softmax_columns(scores):
    peak = jnp.max(scores, axis=0, keepdims=True)
    powers = jnp.exp(scores - peak)
    return powers * (1.0 / jnp.sum(powers, axis=0, keepdims=True))


def short_units(rows):
    for index in range(GROUPS):
        for block in range(rows // BLOCK):
            start = window_start(block, rows)
            yield (
                index, block, slice(index * WIDE, (index + 1) * WIDE),
                slice(block * BLOCK, (block + 1) * BLOCK), slice(start, start + WINDOW),
            )


def short_attention(queries, keys, values, bias, context, shares, rows):
    def task(index, block, columns, own, window):
        def products():
            return nt(keys[window, columns], stack_heads(queries[own, columns]))

        def rest(scores):
            exact = softmax_columns(scores + jnp.concatenate([bias[block]] * STACK, axis=1))
            if shares is not None:
                shares[index, block] = exact
            mixed = tn(exact.astype(bf16), values[window, columns])
            context[own, columns] = unstack_heads(mixed).astype(bf16)

        return products, rest

    run_tasks([task(*unit) for unit in short_units(rows)])


def short_attention_back(queries, keys, values, dcontext, shares, dqueries, dkeys, dvalues, rows):
    dkeys[...] = jnp.zeros_like(dkeys)
    dvalues[...] = jnp.zeros_like(dvalues)

    def task(index, block, columns, own, window):
        def products():
            dstacked = stack_heads(dcontext[own, columns])
            return dstacked, nt(values[window, columns], dstacked)

        def rest(value):
            dstacked, dshares = value
            exact = shares[index, block]
            inner = jnp.sum(exact * dshares, axis=0, keepdims=True)
            dscores = (exact * (dshares - inner)).astype(bf16)
            mixed = tn(dscores, keys[window, columns])
            dqueries[own, columns] = (unstack_heads(mixed) * head_scale).astype(bf16)
            dkeys[window, columns] += nn(dscores, stack_heads(queries[own, columns]))
            dvalues[window, columns] += nn(exact.astype(bf16), dstacked)

        return products, rest

    run_tasks([task(*unit) for unit in short_units(rows)])


def project_to(tokens, low, weight, extra, scale=None):
    value = nn(tokens, weight)
    if extra is not None:
        value = value + nn(low, extra)
    value = value.astype(bf16)
    return value if scale is None else value * jnp.asarray(scale, bf16)


def dense_tasks(tokens, context, weights, gains, hidden, out, kept=None, ready=None):
    out_weight, inner_weight, outer_weight = weights
    attention_gain, output_gain = gains
    rows, width = tokens.shape
    halves = [slice(0, rows // 2), slice(rows // 2, rows)]
    chunks = [slice(start, start + CHUNK) for start in range(0, hidden.shape[1], CHUNK)]
    ready = ready or {}
    unit, inverse = (kept["unit"], kept["inverse"]) if kept else (ready["unit"], None)
    low = out

    def wait(name):
        if name in ready:
            ready.pop(name)()

    def attend_out(r):
        def products():
            wait("out")
            return nn(context[r, :], out_weight[...])

        def rest(value):
            scaled, factor = normalize(tokens[r, :].astype(f32) + value)
            if kept:
                inverse[r, :] = factor
                unit[r, :] = scaled
                low[r, :] = (scaled * attention_gain).astype(bf16)
            else:
                middle = scaled * attention_gain
                unit[r, :] = middle
                low[r, :] = middle.astype(bf16)

        return products, rest

    def inner_part(r, columns):
        def products():
            wait(("inner", columns.start))
            return nn(low[r, :], inner_weight[:, columns])

        def rest(inner):
            phi = 0.5 + 0.5 * lax.erf(inner * 0.7071067811865476)
            hidden[r, columns] = (inner * phi).astype(bf16)
            if kept:
                kept["slope"][r, columns] = phi + inner * (
                    jnp.exp(-0.5 * inner * inner) * 0.3989422804014327
                )

        return products, rest

    def outer_part(r):
        def products():
            wait("outer")
            return nn(hidden[r, :], outer_weight[...])

        def rest(value):
            middle = unit[r, :] * attention_gain if kept else unit[r, :]
            scaled, factor = normalize(middle + value)
            out[r, :] = (scaled * output_gain).astype(bf16)
            if kept:
                dsecond = normalize_back(kept["cotangent"][r, :] * output_gain, scaled, factor)
                kept["dfirst"][r, :] = dsecond
                kept["dlow"][r, :] = dsecond.astype(bf16)

        return products, rest

    def outer_back(r, columns):
        def products():
            return nt(kept["dlow"][r, :], outer_weight[columns, :])

        def rest(dhidden):
            hidden[r, columns] = (dhidden * kept["slope"][r, columns]).astype(bf16)

        return products, rest

    def inner_back(r):
        def products():
            return nt(hidden[r, :], inner_weight[...])

        def rest(value):
            dmiddle = kept["dfirst"][r, :] + value
            dfirst = normalize_back(dmiddle * attention_gain, unit[r, :], inverse[r, :])
            kept["dfirst"][r, :] = dfirst
            kept["dlow"][r, :] = dfirst.astype(bf16)

        return products, rest

    def attend_back(r):
        def products():
            return nt(kept["dlow"][r, :], out_weight[...])

        def rest(value):
            kept["dcontext"][r, :] = value.astype(bf16)

        return products, rest

    tasks = [attend_out(r) for r in halves]
    tasks += [inner_part(r, columns) for r in halves for columns in chunks]
    tasks += [outer_part(r) for r in halves]
    if kept:
        tasks += [outer_back(r, columns) for r in halves for columns in chunks]
        tasks += [inner_back(r) for r in halves]
        tasks += [attend_back(r) for r in halves]
    return tasks


class Copies:
    def __init__(self, semaphores):
        self.semaphores = semaphores
        self.count = 0

    def start(self, source, target):
        copy = pltpu.make_async_copy(source, target, self.semaphores.at[self.count])
        self.count += 1
        copy.start()
        return copy


def start_all(copies, pairs):
    return [copies.start(source, target) for source, target in pairs]


def short_kernel(
    lengths, query_down, query_up, value_down, value_up, attention_gain_in, output_gain_in,
    tokens_in, cotangent_in, query_in, key_in, value_in, out_in, inner_in, outer_in,
    out_out, grad_out, up_out, factors_out,
    tokens, cotangent, query_weight, key_weight, value_weight, out_weight, inner_weight, outer_weight,
    down, query_rows, value_rows, bias, queries, keys, values, context, shares,
    unit, inverse, dfirst, slope, hidden, out, dlow, semaphores,
):
    rows, width = tokens.shape
    copies = Copies(semaphores)
    waits = start_all(
        copies,
        (
            (tokens_in, tokens), (query_in, query_weight), (key_in, key_weight), (value_in, value_weight),
        ),
    )
    fill_factors(query_down, value_down, query_up, value_up, down, query_rows, value_rows)
    segment_bias(lengths, bias, rows)
    gains = (attention_gain_in[...].reshape(1, width), output_gain_in[...].reshape(1, width))
    waits[0].wait()
    low = nt(tokens[...], down[...]).astype(bf16)
    waits[1].wait()
    queries[...] = project_to(tokens[...], low, query_weight[...], query_rows[...], head_scale)
    waits[2].wait()
    waits[3].wait()
    waits += start_all(
        copies,
        (
            (out_in, out_weight), (inner_in, inner_weight), (outer_in, outer_weight), (cotangent_in, cotangent),
        ),
    )
    keys[...] = project_to(tokens[...], low, key_weight[...], None)
    values[...] = project_to(tokens[...], low, value_weight[...], value_rows[...])
    short_attention(queries, keys, values, bias, context, shares, rows)
    for wait in waits[4:]:
        wait.wait()
    dense = (out_weight, inner_weight, outer_weight)
    dcontext = context
    kept = dict(
        unit=unit, inverse=inverse, dfirst=dfirst, slope=slope, dlow=dlow, cotangent=cotangent, dcontext=dcontext,
    )
    run_tasks(dense_tasks(tokens, context, dense, gains, hidden, out, kept))
    sent = [copies.start(out, out_out)]
    for packed, room in factor_pairs(factors_out, (down, query_rows, value_rows)):
        sent.append(copies.start(room, packed))
    dqueries = hidden.at[:, 0:width]
    dkeys, dvalues = slope.at[:, 0:width], slope.at[:, width : 2 * width]
    short_attention_back(queries, keys, values, dcontext, shares, dqueries, dkeys, dvalues, rows)
    dquery = dqueries[...]
    dkey = dkeys[...].astype(bf16)
    dvalue = dvalues[...].astype(bf16)
    low = nt(tokens[...], down[...]).astype(bf16)
    dlatent = (nt(dquery, query_rows[...]) + nt(dvalue, value_rows[...])).astype(bf16)
    cotangent[...] = (
        dfirst[...]
        + nt(dquery, query_weight[...])
        + nt(dkey, key_weight[...])
        + nt(dvalue, value_weight[...])
        + nn(dlatent, down[...])
    )
    sent.append(copies.start(cotangent, grad_out))
    up_out[0:RANK, :] = adapter_scale * tn(low, dquery)[0:RANK, :]
    up_out[RANK : 2 * RANK, :] = adapter_scale * tn(low, dvalue)[RANK : 2 * RANK, :]
    for copy in sent:
        copy.wait()


def long_kernel(
    lengths_in, factors_in, attention_gain_in, output_gain_in, short_up_in,
    tokens_in, far_in, cotangent_in, query_in, key_in, value_in, out_in, inner_in, outer_in,
    out_out, near_out, far_out, up_out,
    tokens, far, cotangent, query_weight, key_weight, value_weight, out_weight, inner_weight, outer_weight,
    down, query_rows, value_rows, queries, keys, values, context, shares,
    unit, inverse, dfirst, slope, hidden, out, dlow, low, lengths, gain, gain_out, short_up, semaphores,
):
    rows, width = tokens.shape
    items = lengths.shape[0]
    half = rows // items
    copies = Copies(semaphores)
    small = start_all(
        copies,
        (
            *factor_pairs(factors_in, (down, query_rows, value_rows)), (lengths_in, lengths),
            (attention_gain_in, gain), (output_gain_in, gain_out), (short_up_in, short_up),
        ),
    )
    waits = start_all(
        copies,
        (
            (tokens_in, tokens), (query_in, query_weight), (far_in, far), (key_in, key_weight),
            (value_in, value_weight),
        ),
    )
    clear_tails((down, query_rows, value_rows))
    place = lax.axis_index("blk")

    def part(item, which):
        start = 2 * item * half + (place if which == 0 else 1 - place) * half
        return pl.ds(pl.multiple_of(start, half), half)

    def put(target, which, value):
        for item in range(items):
            target[part(item, which), :] = value[item * half : (item + 1) * half]

    for wait in small:
        wait.wait()
    gains = (gain[...].reshape(1, width), gain_out[...].reshape(1, width))
    waits[0].wait()
    low[0:rows, :] = nt(tokens[...], down[...]).astype(bf16)
    waits[1].wait()
    queries[...] = project_to(tokens[...], low[0:rows, :], query_weight[...], query_rows[...], head_scale)
    waits[2].wait()
    low[rows:, :] = nt(far[...], down[...]).astype(bf16)
    waits[3].wait()
    put(keys, 0, project_to(tokens[...], None, key_weight[...], None))
    put(keys, 1, project_to(far[...], None, key_weight[...], None))
    waits[4].wait()
    waits += start_all(
        copies,
        (
            (out_in, out_weight), (inner_in, inner_weight), (outer_in, outer_weight), (cotangent_in, cotangent),
        ),
    )
    put(values, 0, project_to(tokens[...], low[0:rows, :], value_weight[...], value_rows[...]))
    put(values, 1, project_to(far[...], low[rows:, :], value_weight[...], value_rows[...]))

    units = [
        (
            item * GROUPS + index, item, slice(index * WIDE, (index + 1) * WIDE),
            slice(item * half, (item + 1) * half), slice(2 * item * half, 2 * (item + 1) * half),
        )
        for item in range(items)
        for index in range(GROUPS)
    ]
    place_in_half = lax.broadcasted_iota(jnp.int32, (half, LANES), 0) + half
    masks = []
    for item in range(items):
        mask = jnp.where(place_in_half < lengths[item], 0.0, masked_score)
        masks.append(jnp.concatenate([mask] * (STACK * half // LANES), axis=1))

    def forward(number, item, columns, own, joined):
        def products():
            return nt(keys[joined, columns], stack_heads(queries[own, columns]))

        def rest(scores):
            scores = jnp.concatenate([scores[0:half], scores[half:] + masks[item]], axis=0)
            exact = softmax_columns(scores).astype(bf16)
            shares[number] = exact
            turned = jnp.swapaxes(values[joined, columns], 0, 1)
            context[own, columns] = join_heads(turned, exact, half).astype(bf16)

        return products, rest

    run_tasks([forward(*unit_) for unit_ in units])
    for wait in waits[5:]:
        wait.wait()
    dense = (out_weight, inner_weight, outer_weight)
    dcontext = context
    kept = dict(
        unit=unit, inverse=inverse, dfirst=dfirst, slope=slope, dlow=dlow, cotangent=cotangent, dcontext=dcontext,
    )
    run_tasks(dense_tasks(tokens, context, dense, gains, hidden, out, kept))
    sent = [copies.start(out, out_out)]
    dqueries = dlow
    dkeys = hidden.at[:, 0 : 2 * width]
    dvalues = hidden.at[:, 2 * width : 4 * width]

    def backward(number, item, columns, own, joined):
        def products():
            dstacked = stack_heads(dcontext[own, columns])
            return dstacked, nt(values[joined, columns], dstacked)

        def rest(value):
            dstacked, dshares = value
            exact = shares[number].astype(f32)
            inner = jnp.sum(exact * dshares, axis=0, keepdims=True)
            dscores = (exact * (dshares - inner)).astype(bf16)
            turned = jnp.swapaxes(keys[joined, columns], 0, 1)
            dqueries[own, columns] = (join_heads(turned, dscores, half) * head_scale).astype(bf16)
            dkey = nn(dscores, stack_heads(queries[own, columns])).astype(bf16)
            dvalue = nn(shares[number], dstacked).astype(bf16)
            for which in range(2):
                rows_ = slice(which * half, (which + 1) * half)
                target = slice(which * width + columns.start, which * width + columns.stop)
                dkeys[own, target] = dkey[rows_]
                dvalues[own, target] = dvalue[rows_]

        return products, rest

    run_tasks([backward(*unit_) for unit_ in units])

    def back_part(which):
        start = pl.multiple_of((place if which == 0 else 1 - place) * width, LANES)
        return dkeys[:, pl.ds(start, width)], dvalues[:, pl.ds(start, width)]

    dkey, dvalue = back_part(1)
    dlatent = nt(dvalue, value_rows[...]).astype(bf16)
    unit[...] = nt(dkey, key_weight[...]) + nt(dvalue, value_weight[...]) + nn(dlatent, down[...])
    sent.append(copies.start(unit, far_out))
    up = tn(low[rows:, :], dvalue)[RANK : 2 * RANK, :]
    dquery = dqueries[...]
    dkey, dvalue = back_part(0)
    dlatent = (nt(dquery, query_rows[...]) + nt(dvalue, value_rows[...])).astype(bf16)
    cotangent[...] = (
        dfirst[...]
        + nt(dquery, query_weight[...])
        + nt(dkey, key_weight[...])
        + nt(dvalue, value_weight[...])
        + nn(dlatent, down[...])
    )
    sent.append(copies.start(cotangent, near_out))
    up = up + tn(low[0:rows, :], dvalue)[RANK : 2 * RANK, :]
    up_out[0:RANK, :] = adapter_scale * tn(low[0:rows, :], dquery)[0:RANK, :] + short_up[0:RANK, :]
    up_out[RANK : 2 * RANK, :] = adapter_scale * up + short_up[RANK : 2 * RANK, :]
    for copy in sent:
        copy.wait()


def eval_attention_kernel(
    lengths_in, factors_in, after,
    tokens_in, query_in, key_in, value_in,
    context,
    tokens, query_weight, key_weight, value_weight,
    down, query_rows, value_rows, bias, queries, keys, values, lengths, semaphores,
):
    rows, width = tokens.shape
    copies = Copies(semaphores)
    small = start_all(
        copies, ((lengths_in, lengths), *factor_pairs(factors_in, (down, query_rows, value_rows)))
    )
    waits = start_all(
        copies,
        (
            (tokens_in, tokens), (key_in, key_weight), (query_in, query_weight), (value_in, value_weight),
        ),
    )
    clear_tails((down, query_rows, value_rows))
    for wait in small:
        wait.wait()
    segment_bias(lengths, bias, rows)
    waits[0].wait()
    waits[1].wait()
    keys[...] = project_to(tokens[...], None, key_weight[...], None)
    waits[2].wait()
    merged = (query_weight[...].astype(f32) + tn(down[...], query_rows[...])).astype(bf16)
    queries[...] = project_to(tokens[...], None, merged, None, head_scale)
    waits[3].wait()
    merged = (value_weight[...].astype(f32) + tn(down[...], value_rows[...])).astype(bf16)
    values[...] = project_to(tokens[...], None, merged, None)
    short_attention(queries, keys, values, bias, context, None, rows)


def eval_dense_kernel(
    attention_gain_in, output_gain_in, after,
    tokens_in, context_in, out_in, inner_in, outer_in, near_in, far_in,
    out_out, grad_out,
    tokens, context, out_weight, inner_weight, outer_weight, near, far, unit, hidden, gain, gain_out, semaphores,
):
    width = tokens.shape[1]
    copies = Copies(semaphores)
    first = start_all(
        copies,
        (
            (attention_gain_in, gain), (output_gain_in, gain_out),
            (context_in, context), (out_in, out_weight), (tokens_in, tokens),
        ),
    )
    inner = {}
    for start in range(0, hidden.shape[1], CHUNK):
        columns = slice(start, start + CHUNK)
        inner[start] = copies.start(inner_in.at[:, columns], inner_weight.at[:, columns])
    outer, *last = start_all(copies, ((outer_in, outer_weight), (near_in, near), (far_in, far)))
    ready = {("inner", start): copy.wait for start, copy in inner.items()}
    ready["outer"] = outer.wait
    ready["unit"] = unit
    for wait in first:
        wait.wait()
    gains = (gain[...].reshape(1, width), gain_out[...].reshape(1, width))
    dense = (out_weight, inner_weight, outer_weight)
    run_tasks(dense_tasks(tokens, context, dense, gains, hidden, out_out, None, ready))
    for wait in last:
        wait.wait()
    near[...] = near[...] + far[...]
    copies.start(near, grad_out).wait()


IN_VMEM = pl.BlockSpec(memory_space=pltpu.VMEM)
IN_SMEM = pl.BlockSpec(memory_space=pltpu.SMEM)
ANYWHERE = pl.BlockSpec(memory_space=pl.ANY)
FACTORS = [IN_VMEM] * 4


def kernel_call(kernel, in_specs, out_specs, out_shape, scratch, copies, flops, moved, name):
    return pl.pallas_call(
        kernel,
        in_specs=in_specs,
        out_specs=out_specs,
        out_shape=out_shape,
        scratch_shapes=[*scratch, pltpu.SemaphoreType.DMA((copies,))],
        compiler_params=pltpu.CompilerParams(vmem_limit_bytes=VMEM_LIMIT),
        cost_estimate=pl.CostEstimate(flops=int(flops), bytes_accessed=int(moved), transcendentals=0),
        name=name,
    )


def shape(dims, kind):
    return jax.ShapeDtypeStruct(dims, kind)


def vm(dims, kind):
    return pltpu.VMEM(dims, kind)


def weight_room(width, wide):
    square = vm((width, width), bf16)
    return [square, square, square, square, vm((width, wide), bf16), vm((wide, width), bf16)]


def factor_room(width):
    return [vm((LANES, width), bf16)] * 3


def kept_room(rows, width, wide):
    return [
        vm((rows, width), f32), vm((rows, 1), f32), vm((rows, width), f32),
        vm((rows, wide), f32), vm((rows, wide), bf16), vm((rows, width), bf16), vm((rows, width), bf16),
    ]


def partner(value, axis, mask):
    count = lax.axis_size(axis)
    return lax.ppermute(value, axis, [(i, i ^ mask) for i in range(count)])


def quad_parts(value, axis, bit):
    masks = [mask * bit for mask in (1, 2, 3) if mask * bit < lax.axis_size(axis)]
    return [value, *[partner(value, axis, mask) for mask in masks]]


def add_up(parts):
    return functools.reduce(lambda a, b: a + b, parts)


def run_short(lengths, factors, gains, tokens, cotangent, weights):
    rows, width = tokens.shape
    wide = weights[4].shape[1]
    blocks = rows // BLOCK
    return kernel_call(
        short_kernel,
        [IN_SMEM, *FACTORS, IN_VMEM, IN_VMEM, *[ANYWHERE] * 8],
        [ANYWHERE, ANYWHERE, IN_VMEM, ANYWHERE],
        [
            shape((rows, width), bf16), shape((rows, width), f32), shape((2 * RANK, width), f32),
            shape((6 * RANK, width), bf16),
        ],
        [
            vm((rows, width), bf16), vm((rows, width), f32), *weight_room(width, wide), *factor_room(width),
            vm((blocks, WINDOW, BLOCK), f32), *[vm((rows, width), bf16)] * 4,
            vm((GROUPS, blocks, WINDOW, STACK * BLOCK), f32), *kept_room(rows, width, wide),
        ],
        16, 20e9, 25e6, "short_step",
    )(lengths, *factors, *gains, tokens, cotangent, *weights)


def run_long(lengths, factors, gains, short_up, tokens, far, cotangent, weights):
    rows, width = tokens.shape
    wide = weights[4].shape[1]
    items = lengths.shape[0]
    half = rows // items
    return kernel_call(
        long_kernel,
        [ANYWHERE] * 14,
        [ANYWHERE, ANYWHERE, ANYWHERE, IN_VMEM],
        [
            shape((rows, width), bf16), shape((rows, width), f32), shape((rows, width), f32),
            shape((2 * RANK, width), f32),
        ],
        [
            vm((rows, width), bf16), vm((rows, width), bf16), vm((rows, width), f32),
            *weight_room(width, wide), *factor_room(width), vm((rows, width), bf16),
            *[vm((2 * rows, width), bf16)] * 2, vm((rows, width), bf16),
            vm((items * GROUPS, 2 * half, STACK * half), bf16), *kept_room(rows, width, wide),
            vm((2 * rows, LANES), bf16), pltpu.SMEM((items,), jnp.int32), vm((width,), f32), vm((width,), f32),
            vm((2 * RANK, width), f32),
        ],
        20, 22e9, 30e6, "long_step",
    )(lengths, factors, *gains, short_up, tokens, far, cotangent, *weights)


def run_eval_attention(lengths, factors, after, tokens, weights):
    rows, width = tokens.shape
    blocks = rows // BLOCK
    return kernel_call(
        eval_attention_kernel,
        [ANYWHERE] * 7,
        IN_VMEM,
        shape((rows, width), bf16),
        [
            vm((rows, width), bf16), *[vm((width, width), bf16)] * 3, *factor_room(width),
            vm((blocks, WINDOW, BLOCK), f32), *[vm((rows, width), bf16)] * 3,
            pltpu.SMEM(lengths.shape, jnp.int32),
        ],
        8, 4e9, 6e6, "eval_attention",
    )(lengths, factors, after, tokens, *weights[0:3])


def run_eval_dense(gains, after, tokens, context, weights, near, far):
    rows, width = tokens.shape
    wide = weights[4].shape[1]
    return kernel_call(
        eval_dense_kernel,
        [ANYWHERE] * 10,
        [IN_VMEM, ANYWHERE],
        [shape((rows, width), bf16), shape((rows, width), f32)],
        [
            vm((rows, width), bf16), vm((rows, width), bf16), *weight_room(width, wide)[3:],
            vm((rows, width), f32), vm((rows, width), f32), vm((rows, width), f32), vm((rows, wide), bf16),
            vm((width,), f32), vm((width,), f32),
        ],
        12, 6e9, 18e6, "eval_dense",
    )(*gains, after, tokens, context, *weights[3:], near, far)


def body(
    short_tokens, short_lengths, long_tokens, long_lengths, eval_tokens, eval_lengths,
    query_matrix, key_weight, value_matrix, out_weight, inner_weight, outer_weight,
    query_down_factor, query_up_factor, value_down_factor, value_up_factor,
    attention_gain, output_gain, cot_short, cot_long,
):
    items, half, width = long_tokens.shape
    factors = (query_down_factor.T, query_up_factor, value_down_factor.T, value_up_factor)
    gains = (attention_gain, output_gain)
    weights = (query_matrix, key_weight, value_matrix, out_weight, inner_weight, outer_weight)

    long_flat = long_tokens.reshape(items * half, width)
    far_flat = partner(long_flat, "blk", 1)
    short_out, short_grad, short_up, packed = run_short(
        short_lengths, factors, gains, short_tokens, cot_short, weights
    )
    long_out, near_grad, far_grad, up = run_long(
        long_lengths, packed, gains, short_up, long_flat, far_flat,
        cot_long.reshape(items * half, width), weights,
    )
    up = up + partner(up, "blk", 1)
    up, far_grad = lax.optimization_barrier((up, far_grad))
    arrived = partner(far_grad, "blk", 1)

    stages = []
    bit = 1
    while bit < lax.axis_size("dp"):
        stages.append(bit)
        bit *= 4
    parts = quad_parts(up, "dp", stages[0])
    context = run_eval_attention(eval_lengths, packed, up, eval_tokens, weights)
    context, *parts = lax.optimization_barrier((context, *parts))
    first_sum = add_up(parts)
    for bit in stages[1:]:
        parts = quad_parts(add_up(parts), "dp", bit)
    eval_out, long_grad = run_eval_dense(
        gains, first_sum, eval_tokens, context, weights, near_grad, arrived
    )
    eval_out, *parts = lax.optimization_barrier((eval_out, *parts))
    query_up_grad = add_up([part[0:RANK] for part in parts])
    value_up_grad = add_up([part[RANK:] for part in parts])

    return (
        short_out,
        long_out.reshape(items, half, width),
        short_grad,
        long_grad.reshape(items, half, width),
        query_up_grad,
        value_up_grad,
        eval_out,
    )


def solution(mesh):
    rows = P(("dp", "blk"), None)
    items = P("dp", "blk", None)
    return jax.shard_map(
        body,
        mesh=mesh,
        in_specs=(
            rows, rows, items, P("dp"), rows, rows, *[P()] * 12, rows, items,
        ),
        out_specs=(rows, items, rows, items, P(), P(), rows),
        check_vma=False,
    )
```

```python
import functools

import jax
import jax.numpy as jnp
from jax import lax
from jax.experimental import pallas as pl
from jax.experimental.pallas import tpu as pltpu
from jax.sharding import PartitionSpec as P

HEADS = 12
HEAD = 64
STACK = 4
WIDE = STACK * HEAD
GROUPS = HEADS // STACK
BLOCK = 128
WINDOW = 256
REACH = 64
LANES = 128
RANK = 8
VMEM_LIMIT = 62 * 2**20
CHUNK = 1024

adapter_scale = 2.0
norm_eps = 1e-05
masked_score = -1000000000.0
head_scale = HEAD ** (-0.5)

bf16 = jnp.bfloat16
f32 = jnp.float32


def nn(left, right):
    return jnp.dot(left, right, preferred_element_type=f32)


def nt(left, right):
    return lax.dot_general(left, right, (((1,), (1,)), ((), ())), preferred_element_type=f32)


def tn(left, right):
    return lax.dot_general(left, right, (((0,), (0,)), ((), ())), preferred_element_type=f32)


def fill_factors(query_down, value_down, query_up, value_up, down, query_rows, value_rows):
    width = down.shape[1]
    blank = jnp.zeros((RANK, width), f32)
    rest = jnp.zeros((LANES - 2 * RANK, width), bf16)
    query_two = adapter_scale * query_up[...].astype(f32)
    value_two = adapter_scale * value_up[...].astype(f32)
    both = [query_down[...].astype(f32), value_down[...].astype(f32)]
    for target, parts in (
        (down, both), (query_rows, [query_two, blank]), (value_rows, [blank, value_two]),
    ):
        target[0 : 2 * RANK, :] = jnp.concatenate(parts, axis=0).astype(bf16)
        target[2 * RANK :, :] = rest


def factor_pairs(factors, rooms):
    size = 2 * RANK
    return [
        (factors.at[i * size : (i + 1) * size, :], room.at[0:size, :]) for i, room in enumerate(rooms)
    ]


def clear_tails(rooms):
    for room in rooms:
        room[2 * RANK :, :] = jnp.zeros((LANES - 2 * RANK, room.shape[1]), bf16)


def head_masks():
    lane = lax.broadcasted_iota(jnp.int32, (1, WIDE), 1)
    return [(lane >= h * HEAD) & (lane < (h + 1) * HEAD) for h in range(STACK)]


def stack_heads(value):
    zero = jnp.zeros_like(value)
    return jnp.concatenate([jnp.where(mask, value, zero) for mask in head_masks()], axis=0)


def unstack_heads(value):
    rows = value.shape[0] // STACK
    lane = lax.broadcasted_iota(jnp.int32, (1, LANES), 1)
    low = lane < HEAD
    parts = []
    for pair in range(STACK // 2):
        columns = slice(pair * LANES, (pair + 1) * LANES)
        first = value[2 * pair * rows : (2 * pair + 1) * rows, columns]
        second = value[(2 * pair + 1) * rows : (2 * pair + 2) * rows, columns]
        parts.append(jnp.where(low, first, second))
    return jnp.concatenate(parts, axis=1)


def join_heads(turned, right, count):
    parts = [
        nn(turned[h * HEAD : (h + 1) * HEAD], right[:, h * count : (h + 1) * count]) for h in range(STACK)
    ]
    return jnp.swapaxes(jnp.concatenate(parts, axis=0), 0, 1)


def normalize(value):
    centre = value - jnp.mean(value, axis=-1, keepdims=True)
    inverse = lax.rsqrt(jnp.mean(centre * centre, axis=-1, keepdims=True) + norm_eps)
    return centre * inverse, inverse


def normalize_back(grad, unit, inverse):
    return inverse * (
        grad
        - jnp.mean(grad, axis=-1, keepdims=True)
        - unit * jnp.mean(grad * unit, axis=-1, keepdims=True)
    )


def segment_bias(lengths, bias, rows):
    key_place = lax.broadcasted_iota(jnp.int32, (rows, LANES), 0)
    query_place = lax.broadcasted_iota(jnp.int32, (8, rows), 1)
    key_segment = jnp.zeros((rows, LANES), jnp.int32)
    query_segment = jnp.zeros((8, rows), jnp.int32)
    end = jnp.int32(0)
    for item in range(lengths.shape[1]):
        end = end + lengths[0, item]
        key_segment = key_segment + (key_place >= end).astype(jnp.int32)
        query_segment = query_segment + (query_place >= end).astype(jnp.int32)
    for block in range(rows // BLOCK):
        start = window_start(block, rows)
        same = (
            key_segment[start : start + WINDOW, :]
            == query_segment[0:1, block * BLOCK : (block + 1) * BLOCK]
        )
        bias[block] = jnp.where(same, 0.0, masked_score)


def window_start(block, rows):
    return min(max(block * BLOCK - REACH, 0), rows - WINDOW)


def run_tasks(tasks):
    rest = None
    for products, after in tasks:
        value = products()
        if rest is not None:
            rest()
        rest = functools.partial(after, value)
    rest()


def softmax_columns(scores):
    peak = jnp.max(scores, axis=0, keepdims=True)
    powers = jnp.exp(scores - peak)
    return powers * (1.0 / jnp.sum(powers, axis=0, keepdims=True))


def short_units(rows):
    for index in range(GROUPS):
        for block in range(rows // BLOCK):
            start = window_start(block, rows)
            yield (
                index, block, slice(index * WIDE, (index + 1) * WIDE),
                slice(block * BLOCK, (block + 1) * BLOCK), slice(start, start + WINDOW),
            )


def short_attention(queries, keys, values, bias, context, shares, rows):
    def task(index, block, columns, own, window):
        def products():
            return nt(keys[window, columns], stack_heads(queries[own, columns]))

        def rest(scores):
            exact = softmax_columns(scores + jnp.concatenate([bias[block]] * STACK, axis=1))
            if shares is not None:
                shares[index, block] = exact
            mixed = tn(exact.astype(bf16), values[window, columns])
            context[own, columns] = unstack_heads(mixed).astype(bf16)

        return products, rest

    run_tasks([task(*unit) for unit in short_units(rows)])


def short_attention_back(queries, keys, values, dcontext, shares, dqueries, dkeys, dvalues, rows):
    dkeys[...] = jnp.zeros_like(dkeys)
    dvalues[...] = jnp.zeros_like(dvalues)

    def task(index, block, columns, own, window):
        def products():
            dstacked = stack_heads(dcontext[own, columns])
            return dstacked, nt(values[window, columns], dstacked)

        def rest(value):
            dstacked, dshares = value
            exact = shares[index, block]
            inner = jnp.sum(exact * dshares, axis=0, keepdims=True)
            dscores = (exact * (dshares - inner)).astype(bf16)
            mixed = tn(dscores, keys[window, columns])
            dqueries[own, columns] = (unstack_heads(mixed) * head_scale).astype(bf16)
            dkeys[window, columns] += nn(dscores, stack_heads(queries[own, columns]))
            dvalues[window, columns] += nn(exact.astype(bf16), dstacked)

        return products, rest

    run_tasks([task(*unit) for unit in short_units(rows)])


def project_to(tokens, low, weight, extra, scale=None):
    value = nn(tokens, weight)
    if extra is not None:
        value = value + nn(low, extra)
    value = value.astype(bf16)
    return value if scale is None else value * jnp.asarray(scale, bf16)


def dense_tasks(tokens, context, weights, gains, hidden, out, kept=None, ready=None):
    out_weight, inner_weight, outer_weight = weights
    attention_gain, output_gain = gains
    rows, width = tokens.shape
    count = 2 if kept else 4
    halves = [slice(i * rows // count, (i + 1) * rows // count) for i in range(count)]
    chunks = [slice(start, start + CHUNK) for start in range(0, hidden.shape[1], CHUNK)]
    ready = ready or {}
    unit, inverse = (kept["unit"], kept["inverse"]) if kept else (ready["unit"], None)
    low = out

    def wait(name):
        if name in ready:
            ready.pop(name)()

    def attend_out(r):
        def products():
            wait("out")
            return nn(context[r, :], out_weight[...])

        def rest(value):
            scaled, factor = normalize(tokens[r, :].astype(f32) + value)
            if kept:
                inverse[r, :] = factor
                unit[r, :] = scaled
                low[r, :] = (scaled * attention_gain).astype(bf16)
            else:
                middle = scaled * attention_gain
                unit[r, :] = middle
                low[r, :] = middle.astype(bf16)

        return products, rest

    def inner_part(r, columns):
        def products():
            wait(("inner", columns.start))
            return nn(low[r, :], inner_weight[:, columns])

        def rest(inner):
            phi = 0.5 + 0.5 * lax.erf(inner * 0.7071067811865476)
            hidden[r, columns] = (inner * phi).astype(bf16)
            if kept:
                kept["slope"][r, columns] = phi + inner * (
                    jnp.exp(-0.5 * inner * inner) * 0.3989422804014327
                )

        return products, rest

    def outer_part(r):
        def products():
            wait("outer")
            return nn(hidden[r, :], outer_weight[...])

        def rest(value):
            middle = unit[r, :] * attention_gain if kept else unit[r, :]
            scaled, factor = normalize(middle + value)
            out[r, :] = (scaled * output_gain).astype(bf16)
            if kept:
                dsecond = normalize_back(kept["cotangent"][r, :] * output_gain, scaled, factor)
                kept["dfirst"][r, :] = dsecond
                kept["dlow"][r, :] = dsecond.astype(bf16)

        return products, rest

    def outer_back(r, columns):
        def products():
            return nt(kept["dlow"][r, :], outer_weight[columns, :])

        def rest(dhidden):
            hidden[r, columns] = (dhidden * kept["slope"][r, columns]).astype(bf16)

        return products, rest

    def inner_back(r):
        def products():
            return nt(hidden[r, :], inner_weight[...])

        def rest(value):
            dmiddle = kept["dfirst"][r, :] + value
            dfirst = normalize_back(dmiddle * attention_gain, unit[r, :], inverse[r, :])
            kept["dfirst"][r, :] = dfirst
            kept["dlow"][r, :] = dfirst.astype(bf16)

        return products, rest

    def attend_back(r):
        def products():
            return nt(kept["dlow"][r, :], out_weight[...])

        def rest(value):
            kept["dcontext"][r, :] = value.astype(bf16)

        return products, rest

    tasks = [attend_out(r) for r in halves]
    tasks += [inner_part(r, columns) for r in halves for columns in chunks]
    tasks += [outer_part(r) for r in halves]
    if kept:
        tasks += [outer_back(r, columns) for r in halves for columns in chunks]
        tasks += [inner_back(r) for r in halves]
        tasks += [attend_back(r) for r in halves]
    return tasks


class Copies:
    def __init__(self, semaphores):
        self.semaphores = semaphores
        self.count = 0

    def start(self, source, target):
        copy = pltpu.make_async_copy(source, target, self.semaphores.at[self.count])
        self.count += 1
        copy.start()
        return copy


def start_all(copies, pairs):
    return [copies.start(source, target) for source, target in pairs]


def short_kernel(
    lengths, query_down, query_up, value_down, value_up, attention_gain_in, output_gain_in,
    tokens_in, cotangent_in, query_in, key_in, value_in, out_in, inner_in, outer_in,
    out_out, grad_out, up_out, factors_out,
    tokens, cotangent, query_weight, key_weight, value_weight, out_weight, inner_weight, outer_weight,
    down, query_rows, value_rows, bias, queries, keys, values, context, shares,
    unit, inverse, dfirst, slope, hidden, out, dlow, semaphores,
):
    rows, width = tokens.shape
    copies = Copies(semaphores)
    waits = start_all(
        copies,
        (
            (tokens_in, tokens), (query_in, query_weight), (key_in, key_weight), (value_in, value_weight),
        ),
    )
    fill_factors(query_down, value_down, query_up, value_up, down, query_rows, value_rows)
    segment_bias(lengths, bias, rows)
    gains = (attention_gain_in[...].reshape(1, width), output_gain_in[...].reshape(1, width))
    waits[0].wait()
    low = nt(tokens[...], down[...]).astype(bf16)
    waits[1].wait()
    queries[...] = project_to(tokens[...], low, query_weight[...], query_rows[...], head_scale)
    waits[2].wait()
    waits[3].wait()
    waits += start_all(
        copies,
        (
            (out_in, out_weight), (inner_in, inner_weight), (outer_in, outer_weight), (cotangent_in, cotangent),
        ),
    )
    keys[...] = project_to(tokens[...], low, key_weight[...], None)
    values[...] = project_to(tokens[...], low, value_weight[...], value_rows[...])
    short_attention(queries, keys, values, bias, context, shares, rows)
    for wait in waits[4:]:
        wait.wait()
    dense = (out_weight, inner_weight, outer_weight)
    dcontext = context
    kept = dict(
        unit=unit, inverse=inverse, dfirst=dfirst, slope=slope, dlow=dlow, cotangent=cotangent, dcontext=dcontext,
    )
    run_tasks(dense_tasks(tokens, context, dense, gains, hidden, out, kept))
    sent = [copies.start(out, out_out)]
    for packed, room in factor_pairs(factors_out, (down, query_rows, value_rows)):
        sent.append(copies.start(room, packed))
    dqueries = hidden.at[:, 0:width]
    dkeys, dvalues = slope.at[:, 0:width], slope.at[:, width : 2 * width]
    short_attention_back(queries, keys, values, dcontext, shares, dqueries, dkeys, dvalues, rows)
    dquery = dqueries[...]
    dkey = dkeys[...].astype(bf16)
    dvalue = dvalues[...].astype(bf16)
    low = nt(tokens[...], down[...]).astype(bf16)
    dlatent = (nt(dquery, query_rows[...]) + nt(dvalue, value_rows[...])).astype(bf16)
    for r in (slice(0, rows // 2), slice(rows // 2, rows)):
        cotangent[r, :] = (
            dfirst[r, :]
            + nt(dquery[r], query_weight[...])
            + nt(dkey[r], key_weight[...])
            + nt(dvalue[r], value_weight[...])
            + nn(dlatent[r], down[...])
        )
        sent.append(copies.start(cotangent.at[r, :], grad_out.at[r, :]))
    up_out[0:RANK, :] = adapter_scale * tn(low, dquery)[0:RANK, :]
    up_out[RANK : 2 * RANK, :] = adapter_scale * tn(low, dvalue)[RANK : 2 * RANK, :]
    for copy in sent:
        copy.wait()


def long_kernel(
    lengths_in, factors_in, attention_gain_in, output_gain_in, short_up_in,
    tokens_in, far_in, cotangent_in, query_in, key_in, value_in, out_in, inner_in, outer_in,
    out_out, near_out, far_out, up_out,
    tokens, far, cotangent, query_weight, key_weight, value_weight, out_weight, inner_weight, outer_weight,
    down, query_rows, value_rows, queries, keys, values, context, shares,
    unit, inverse, dfirst, slope, hidden, out, dlow, low, lengths, gain, gain_out, short_up, semaphores,
):
    rows, width = tokens.shape
    items = lengths.shape[0]
    half = rows // items
    copies = Copies(semaphores)
    small = start_all(
        copies,
        (
            *factor_pairs(factors_in, (down, query_rows, value_rows)), (lengths_in, lengths),
            (attention_gain_in, gain), (output_gain_in, gain_out), (short_up_in, short_up),
        ),
    )
    waits = start_all(
        copies,
        (
            (tokens_in, tokens), (query_in, query_weight), (far_in, far), (key_in, key_weight),
            (value_in, value_weight),
        ),
    )
    clear_tails((down, query_rows, value_rows))
    place = lax.axis_index("blk")

    def part(item, which):
        start = 2 * item * half + (place if which == 0 else 1 - place) * half
        return pl.ds(pl.multiple_of(start, half), half)

    def put(target, which, value):
        for item in range(items):
            target[part(item, which), :] = value[item * half : (item + 1) * half]

    for wait in small:
        wait.wait()
    gains = (gain[...].reshape(1, width), gain_out[...].reshape(1, width))
    waits[0].wait()
    low[0:rows, :] = nt(tokens[...], down[...]).astype(bf16)
    waits[1].wait()
    queries[...] = project_to(tokens[...], low[0:rows, :], query_weight[...], query_rows[...], head_scale)
    for wait in waits[2:5]:
        wait.wait()
    waits += start_all(
        copies,
        (
            (out_in, out_weight), (inner_in, inner_weight), (outer_in, outer_weight), (cotangent_in, cotangent),
        ),
    )
    low[rows:, :] = nt(far[...], down[...]).astype(bf16)
    put(keys, 0, project_to(tokens[...], None, key_weight[...], None))
    put(keys, 1, project_to(far[...], None, key_weight[...], None))
    put(values, 0, project_to(tokens[...], low[0:rows, :], value_weight[...], value_rows[...]))
    put(values, 1, project_to(far[...], low[rows:, :], value_weight[...], value_rows[...]))

    units = [
        (
            item * GROUPS + index, item, slice(index * WIDE, (index + 1) * WIDE),
            slice(item * half, (item + 1) * half), slice(2 * item * half, 2 * (item + 1) * half),
        )
        for item in range(items)
        for index in range(GROUPS)
    ]
    place_in_half = lax.broadcasted_iota(jnp.int32, (half, LANES), 0) + half
    masks = []
    for item in range(items):
        mask = jnp.where(place_in_half < lengths[item], 0.0, masked_score)
        masks.append(jnp.concatenate([mask] * (STACK * half // LANES), axis=1))

    def forward(number, item, columns, own, joined):
        def products():
            return nt(keys[joined, columns], stack_heads(queries[own, columns]))

        def rest(scores):
            scores = jnp.concatenate([scores[0:half], scores[half:] + masks[item]], axis=0)
            exact = softmax_columns(scores).astype(bf16)
            shares[number] = exact
            turned = jnp.swapaxes(values[joined, columns], 0, 1)
            context[own, columns] = join_heads(turned, exact, half).astype(bf16)

        return products, rest

    run_tasks([forward(*unit_) for unit_ in units])
    for wait in waits[5:]:
        wait.wait()
    dense = (out_weight, inner_weight, outer_weight)
    dcontext = context
    kept = dict(
        unit=unit, inverse=inverse, dfirst=dfirst, slope=slope, dlow=dlow, cotangent=cotangent, dcontext=dcontext,
    )
    run_tasks(dense_tasks(tokens, context, dense, gains, hidden, out, kept))
    sent = [copies.start(out, out_out)]
    dqueries = dlow
    dkeys = hidden.at[:, 0 : 2 * width]
    dvalues = hidden.at[:, 2 * width : 4 * width]

    def backward(number, item, columns, own, joined):
        def products():
            dstacked = stack_heads(dcontext[own, columns])
            return dstacked, nt(values[joined, columns], dstacked)

        def rest(value):
            dstacked, dshares = value
            exact = shares[number].astype(f32)
            inner = jnp.sum(exact * dshares, axis=0, keepdims=True)
            dscores = (exact * (dshares - inner)).astype(bf16)
            turned = jnp.swapaxes(keys[joined, columns], 0, 1)
            dqueries[own, columns] = (join_heads(turned, dscores, half) * head_scale).astype(bf16)
            dkey = nn(dscores, stack_heads(queries[own, columns])).astype(bf16)
            dvalue = nn(shares[number], dstacked).astype(bf16)
            for which in range(2):
                rows_ = slice(which * half, (which + 1) * half)
                target = slice(which * width + columns.start, which * width + columns.stop)
                dkeys[own, target] = dkey[rows_]
                dvalues[own, target] = dvalue[rows_]

        return products, rest

    run_tasks([backward(*unit_) for unit_ in units])

    def back_part(which):
        start = pl.multiple_of((place if which == 0 else 1 - place) * width, LANES)
        return dkeys[:, pl.ds(start, width)], dvalues[:, pl.ds(start, width)]

    dkey, dvalue = back_part(1)
    dlatent = nt(dvalue, value_rows[...]).astype(bf16)
    unit[...] = nt(dkey, key_weight[...]) + nt(dvalue, value_weight[...]) + nn(dlatent, down[...])
    sent.append(copies.start(unit, far_out))
    up = tn(low[rows:, :], dvalue)[RANK : 2 * RANK, :]
    dquery = dqueries[...]
    dkey, dvalue = back_part(0)
    dlatent = (nt(dquery, query_rows[...]) + nt(dvalue, value_rows[...])).astype(bf16)
    for r in (slice(0, rows // 2), slice(rows // 2, rows)):
        cotangent[r, :] = (
            dfirst[r, :]
            + nt(dquery[r], query_weight[...])
            + nt(dkey[r], key_weight[...])
            + nt(dvalue[r], value_weight[...])
            + nn(dlatent[r], down[...])
        )
        sent.append(copies.start(cotangent.at[r, :], near_out.at[r, :]))
    up = up + tn(low[0:rows, :], dvalue)[RANK : 2 * RANK, :]
    up_out[0:RANK, :] = adapter_scale * tn(low[0:rows, :], dquery)[0:RANK, :] + short_up[0:RANK, :]
    up_out[RANK : 2 * RANK, :] = adapter_scale * up + short_up[RANK : 2 * RANK, :]
    for copy in sent:
        copy.wait()


def eval_attention_kernel(
    lengths_in, factors_in, after,
    tokens_in, query_in, key_in, value_in,
    context,
    tokens, query_weight, key_weight, value_weight,
    down, query_rows, value_rows, bias, queries, keys, values, lengths, semaphores,
):
    rows, width = tokens.shape
    copies = Copies(semaphores)
    small = start_all(
        copies, ((lengths_in, lengths), *factor_pairs(factors_in, (down, query_rows, value_rows)))
    )
    waits = start_all(
        copies,
        (
            (tokens_in, tokens), (key_in, key_weight), (query_in, query_weight), (value_in, value_weight),
        ),
    )
    clear_tails((down, query_rows, value_rows))
    for wait in small:
        wait.wait()
    segment_bias(lengths, bias, rows)
    waits[0].wait()
    waits[1].wait()
    keys[...] = project_to(tokens[...], None, key_weight[...], None)
    waits[2].wait()
    merged = (query_weight[...].astype(f32) + tn(down[...], query_rows[...])).astype(bf16)
    queries[...] = project_to(tokens[...], None, merged, None, head_scale)
    waits[3].wait()
    merged = (value_weight[...].astype(f32) + tn(down[...], value_rows[...])).astype(bf16)
    values[...] = project_to(tokens[...], None, merged, None)
    short_attention(queries, keys, values, bias, context, None, rows)


def eval_dense_kernel(
    attention_gain_in, output_gain_in, after,
    tokens_in, context_in, out_in, inner_in, outer_in, near_in, far_in,
    out_out, grad_out,
    tokens, context, out_weight, inner_weight, outer_weight, near, far, unit, hidden, gain, gain_out, semaphores,
):
    width = tokens.shape[1]
    copies = Copies(semaphores)
    first = start_all(
        copies,
        (
            (attention_gain_in, gain), (output_gain_in, gain_out),
            (context_in, context), (out_in, out_weight), (tokens_in, tokens),
        ),
    )
    inner = {}
    for start in range(0, hidden.shape[1], CHUNK):
        columns = slice(start, start + CHUNK)
        inner[start] = copies.start(inner_in.at[:, columns], inner_weight.at[:, columns])
    outer, *last = start_all(copies, ((outer_in, outer_weight), (near_in, near), (far_in, far)))
    ready = {("inner", start): copy.wait for start, copy in inner.items()}
    ready["outer"] = outer.wait
    ready["unit"] = unit
    for wait in first:
        wait.wait()
    gains = (gain[...].reshape(1, width), gain_out[...].reshape(1, width))
    dense = (out_weight, inner_weight, outer_weight)
    tasks = dense_tasks(tokens, context, dense, gains, hidden, out_out, None, ready)
    sent = []

    def gradient_waits():
        for wait in last:
            wait.wait()

    def gradient_sum(unused):
        near[...] = near[...] + far[...]
        sent.append(copies.start(near, grad_out))

    tasks.insert(len(tasks) - 4, (gradient_waits, gradient_sum))
    run_tasks(tasks)
    sent[0].wait()


IN_VMEM = pl.BlockSpec(memory_space=pltpu.VMEM)
IN_SMEM = pl.BlockSpec(memory_space=pltpu.SMEM)
ANYWHERE = pl.BlockSpec(memory_space=pl.ANY)
FACTORS = [IN_VMEM] * 4


def kernel_call(kernel, in_specs, out_specs, out_shape, scratch, copies, flops, moved, name):
    return pl.pallas_call(
        kernel,
        in_specs=in_specs,
        out_specs=out_specs,
        out_shape=out_shape,
        scratch_shapes=[*scratch, pltpu.SemaphoreType.DMA((copies,))],
        compiler_params=pltpu.CompilerParams(vmem_limit_bytes=VMEM_LIMIT),
        cost_estimate=pl.CostEstimate(flops=int(flops), bytes_accessed=int(moved), transcendentals=0),
        name=name,
    )


def shape(dims, kind):
    return jax.ShapeDtypeStruct(dims, kind)


def vm(dims, kind):
    return pltpu.VMEM(dims, kind)


def weight_room(width, wide):
    square = vm((width, width), bf16)
    return [square, square, square, square, vm((width, wide), bf16), vm((wide, width), bf16)]


def factor_room(width):
    return [vm((LANES, width), bf16)] * 3


def kept_room(rows, width, wide):
    return [
        vm((rows, width), f32), vm((rows, 1), f32), vm((rows, width), f32),
        vm((rows, wide), f32), vm((rows, wide), bf16), vm((rows, width), bf16), vm((rows, width), bf16),
    ]


def partner(value, axis, mask):
    count = lax.axis_size(axis)
    return lax.ppermute(value, axis, [(i, i ^ mask) for i in range(count)])


def quad_parts(value, axis, bit):
    masks = [mask * bit for mask in (1, 2, 3) if mask * bit < lax.axis_size(axis)]
    return [value, *[partner(value, axis, mask) for mask in masks]]


def add_up(parts):
    return functools.reduce(lambda a, b: a + b, parts)


def run_short(lengths, factors, gains, tokens, cotangent, weights):
    rows, width = tokens.shape
    wide = weights[4].shape[1]
    blocks = rows // BLOCK
    return kernel_call(
        short_kernel,
        [IN_SMEM, *FACTORS, IN_VMEM, IN_VMEM, *[ANYWHERE] * 8],
        [ANYWHERE, ANYWHERE, IN_VMEM, ANYWHERE],
        [
            shape((rows, width), bf16), shape((rows, width), f32), shape((2 * RANK, width), f32),
            shape((6 * RANK, width), bf16),
        ],
        [
            vm((rows, width), bf16), vm((rows, width), f32), *weight_room(width, wide), *factor_room(width),
            vm((blocks, WINDOW, BLOCK), f32), *[vm((rows, width), bf16)] * 4,
            vm((GROUPS, blocks, WINDOW, STACK * BLOCK), f32), *kept_room(rows, width, wide),
        ],
        16, 20e9, 25e6, "short_step",
    )(lengths, *factors, *gains, tokens, cotangent, *weights)


def run_long(lengths, factors, gains, short_up, tokens, far, cotangent, weights):
    rows, width = tokens.shape
    wide = weights[4].shape[1]
    items = lengths.shape[0]
    half = rows // items
    return kernel_call(
        long_kernel,
        [ANYWHERE] * 14,
        [ANYWHERE, ANYWHERE, ANYWHERE, IN_VMEM],
        [
            shape((rows, width), bf16), shape((rows, width), f32), shape((rows, width), f32),
            shape((2 * RANK, width), f32),
        ],
        [
            vm((rows, width), bf16), vm((rows, width), bf16), vm((rows, width), f32),
            *weight_room(width, wide), *factor_room(width), vm((rows, width), bf16),
            *[vm((2 * rows, width), bf16)] * 2, vm((rows, width), bf16),
            vm((items * GROUPS, 2 * half, STACK * half), bf16), *kept_room(rows, width, wide),
            vm((2 * rows, LANES), bf16), pltpu.SMEM((items,), jnp.int32), vm((width,), f32), vm((width,), f32),
            vm((2 * RANK, width), f32),
        ],
        20, 22e9, 30e6, "long_step",
    )(lengths, factors, *gains, short_up, tokens, far, cotangent, *weights)


def run_eval_attention(lengths, factors, after, tokens, weights):
    rows, width = tokens.shape
    blocks = rows // BLOCK
    return kernel_call(
        eval_attention_kernel,
        [ANYWHERE] * 7,
        IN_VMEM,
        shape((rows, width), bf16),
        [
            vm((rows, width), bf16), *[vm((width, width), bf16)] * 3, *factor_room(width),
            vm((blocks, WINDOW, BLOCK), f32), *[vm((rows, width), bf16)] * 3,
            pltpu.SMEM(lengths.shape, jnp.int32),
        ],
        8, 4e9, 6e6, "eval_attention",
    )(lengths, factors, after, tokens, *weights[0:3])


def run_eval_dense(gains, after, tokens, context, weights, near, far):
    rows, width = tokens.shape
    wide = weights[4].shape[1]
    return kernel_call(
        eval_dense_kernel,
        [ANYWHERE] * 10,
        [IN_VMEM, ANYWHERE],
        [shape((rows, width), bf16), shape((rows, width), f32)],
        [
            vm((rows, width), bf16), vm((rows, width), bf16), *weight_room(width, wide)[3:],
            vm((rows, width), f32), vm((rows, width), f32), vm((rows, width), f32), vm((rows, wide), bf16),
            vm((width,), f32), vm((width,), f32),
        ],
        12, 6e9, 18e6, "eval_dense",
    )(*gains, after, tokens, context, *weights[3:], near, far)


def body(
    short_tokens, short_lengths, long_tokens, long_lengths, eval_tokens, eval_lengths,
    query_matrix, key_weight, value_matrix, out_weight, inner_weight, outer_weight,
    query_down_factor, query_up_factor, value_down_factor, value_up_factor,
    attention_gain, output_gain, cot_short, cot_long,
):
    items, half, width = long_tokens.shape
    factors = (query_down_factor.T, query_up_factor, value_down_factor.T, value_up_factor)
    gains = (attention_gain, output_gain)
    weights = (query_matrix, key_weight, value_matrix, out_weight, inner_weight, outer_weight)

    long_flat = long_tokens.reshape(items * half, width)
    far_flat = partner(long_flat, "blk", 1)
    short_out, short_grad, short_up, packed = run_short(
        short_lengths, factors, gains, short_tokens, cot_short, weights
    )
    long_out, near_grad, far_grad, up = run_long(
        long_lengths, packed, gains, short_up, long_flat, far_flat,
        cot_long.reshape(items * half, width), weights,
    )
    up = up + partner(up, "blk", 1)
    up, far_grad = lax.optimization_barrier((up, far_grad))
    arrived = partner(far_grad, "blk", 1)

    stages = []
    bit = 1
    while bit < lax.axis_size("dp"):
        stages.append(bit)
        bit *= 4
    parts = quad_parts(up, "dp", stages[0])
    context = run_eval_attention(eval_lengths, packed, up, eval_tokens, weights)
    context, arrived, *parts = lax.optimization_barrier((context, arrived, *parts))
    first_sum = add_up(parts)
    for bit in stages[1:]:
        parts = quad_parts(add_up(parts), "dp", bit)
    eval_out, long_grad = run_eval_dense(
        gains, first_sum, eval_tokens, context, weights, near_grad, arrived
    )
    eval_out, *parts = lax.optimization_barrier((eval_out, *parts))
    query_up_grad = add_up([part[0:RANK] for part in parts])
    value_up_grad = add_up([part[RANK:] for part in parts])

    return (
        short_out,
        long_out.reshape(items, half, width),
        short_grad,
        long_grad.reshape(items, half, width),
        query_up_grad,
        value_up_grad,
        eval_out,
    )


def solution(mesh):
    rows = P(("dp", "blk"), None)
    items = P("dp", "blk", None)
    return jax.shard_map(
        body,
        mesh=mesh,
        in_specs=(
            rows, rows, items, P("dp"), rows, rows, *[P()] * 12, rows, items,
        ),
        out_specs=(rows, items, rows, items, P(), P(), rows),
        check_vma=False,
    )
```

```python
import functools

import jax
import jax.numpy as jnp
from jax import lax
from jax.experimental import pallas as pl
from jax.experimental.pallas import tpu as pltpu
from jax.sharding import PartitionSpec as P

HEADS = 12
HEAD = 64
STACK = 4
WIDE = STACK * HEAD
GROUPS = HEADS // STACK
BLOCK = 128
WINDOW = 256
REACH = 64
LANES = 128
RANK = 8
VMEM_LIMIT = 62 * 2**20
CHUNK = 1024

adapter_scale = 2.0
norm_eps = 1e-05
masked_score = -1000000000.0
head_scale = HEAD ** (-0.5)

bf16 = jnp.bfloat16
f32 = jnp.float32


def nn(left, right):
    return jnp.dot(left, right, preferred_element_type=f32)


def nt(left, right):
    return lax.dot_general(left, right, (((1,), (1,)), ((), ())), preferred_element_type=f32)


def tn(left, right):
    return lax.dot_general(left, right, (((0,), (0,)), ((), ())), preferred_element_type=f32)


def fill_factors(query_down, value_down, query_up, value_up, down, query_rows, value_rows):
    width = down.shape[1]
    blank = jnp.zeros((RANK, width), f32)
    rest = jnp.zeros((LANES - 2 * RANK, width), bf16)
    query_two = adapter_scale * query_up[...].astype(f32)
    value_two = adapter_scale * value_up[...].astype(f32)
    both = [query_down[...].astype(f32), value_down[...].astype(f32)]
    for target, parts in (
        (down, both), (query_rows, [query_two, blank]), (value_rows, [blank, value_two]),
    ):
        target[0 : 2 * RANK, :] = jnp.concatenate(parts, axis=0).astype(bf16)
        target[2 * RANK :, :] = rest


def factor_pairs(factors, rooms):
    size = 2 * RANK
    return [
        (factors.at[i * size : (i + 1) * size, :], room.at[0:size, :]) for i, room in enumerate(rooms)
    ]


def clear_tails(rooms):
    for room in rooms:
        room[2 * RANK :, :] = jnp.zeros((LANES - 2 * RANK, room.shape[1]), bf16)


def head_masks():
    lane = lax.broadcasted_iota(jnp.int32, (1, WIDE), 1)
    return [(lane >= h * HEAD) & (lane < (h + 1) * HEAD) for h in range(STACK)]


def stack_heads(value):
    zero = jnp.zeros_like(value)
    return jnp.concatenate([jnp.where(mask, value, zero) for mask in head_masks()], axis=0)


def unstack_heads(value):
    rows = value.shape[0] // STACK
    lane = lax.broadcasted_iota(jnp.int32, (1, LANES), 1)
    low = lane < HEAD
    parts = []
    for pair in range(STACK // 2):
        columns = slice(pair * LANES, (pair + 1) * LANES)
        first = value[2 * pair * rows : (2 * pair + 1) * rows, columns]
        second = value[(2 * pair + 1) * rows : (2 * pair + 2) * rows, columns]
        parts.append(jnp.where(low, first, second))
    return jnp.concatenate(parts, axis=1)


def join_heads(turned, right, count):
    parts = [
        nn(turned[h * HEAD : (h + 1) * HEAD], right[:, h * count : (h + 1) * count]) for h in range(STACK)
    ]
    return jnp.swapaxes(jnp.concatenate(parts, axis=0), 0, 1)


def normalize(value):
    centre = value - jnp.mean(value, axis=-1, keepdims=True)
    inverse = lax.rsqrt(jnp.mean(centre * centre, axis=-1, keepdims=True) + norm_eps)
    return centre * inverse, inverse


def normalize_back(grad, unit, inverse):
    return inverse * (
        grad
        - jnp.mean(grad, axis=-1, keepdims=True)
        - unit * jnp.mean(grad * unit, axis=-1, keepdims=True)
    )


def segment_bias(lengths, bias, rows):
    key_place = lax.broadcasted_iota(jnp.int32, (rows, LANES), 0)
    query_place = lax.broadcasted_iota(jnp.int32, (8, rows), 1)
    key_segment = jnp.zeros((rows, LANES), jnp.int32)
    query_segment = jnp.zeros((8, rows), jnp.int32)
    end = jnp.int32(0)
    for item in range(lengths.shape[1]):
        end = end + lengths[0, item]
        key_segment = key_segment + (key_place >= end).astype(jnp.int32)
        query_segment = query_segment + (query_place >= end).astype(jnp.int32)
    for block in range(rows // BLOCK):
        start = window_start(block, rows)
        same = (
            key_segment[start : start + WINDOW, :]
            == query_segment[0:1, block * BLOCK : (block + 1) * BLOCK]
        )
        bias[block] = jnp.where(same, 0.0, masked_score)


def window_start(block, rows):
    return min(max(block * BLOCK - REACH, 0), rows - WINDOW)


def run_tasks(tasks):
    rest = None
    for products, after in tasks:
        value = products()
        if rest is not None:
            rest()
        rest = functools.partial(after, value)
    rest()


def softmax_columns(scores):
    peak = jnp.max(scores, axis=0, keepdims=True)
    powers = jnp.exp(scores - peak)
    return powers * (1.0 / jnp.sum(powers, axis=0, keepdims=True))


def short_units(rows):
    for block in range(rows // BLOCK):
        for index in range(GROUPS):
            start = window_start(block, rows)
            yield (
                index, block, slice(index * WIDE, (index + 1) * WIDE),
                slice(block * BLOCK, (block + 1) * BLOCK), slice(start, start + WINDOW),
            )


def short_attention_tasks(queries, keys, values, bias, context, shares, rows):
    def task(index, block, columns, own, window):
        def products():
            return nt(keys[window, columns], stack_heads(queries[own, columns]))

        def rest(scores):
            exact = softmax_columns(scores + jnp.concatenate([bias[block]] * STACK, axis=1))
            if shares is not None:
                shares[index, block] = exact
            mixed = tn(exact.astype(bf16), values[window, columns])
            context[own, columns] = unstack_heads(mixed).astype(bf16)

        return products, rest

    return [task(*unit) for unit in short_units(rows)]


def short_attention_back_tasks(queries, keys, values, dcontext, shares, dqueries, dkeys, dvalues, rows):
    def task(index, block, columns, own, window):
        def products():
            if index == 0 and block == 0:
                dkeys[...] = jnp.zeros_like(dkeys)
                dvalues[...] = jnp.zeros_like(dvalues)
            dstacked = stack_heads(dcontext[own, columns])
            return dstacked, nt(values[window, columns], dstacked)

        def rest(value):
            dstacked, dshares = value
            exact = shares[index, block]
            inner = jnp.sum(exact * dshares, axis=0, keepdims=True)
            dscores = (exact * (dshares - inner)).astype(bf16)
            mixed = tn(dscores, keys[window, columns])
            dqueries[own, columns] = (unstack_heads(mixed) * head_scale).astype(bf16)
            dkeys[window, columns] += nn(dscores, stack_heads(queries[own, columns]))
            dvalues[window, columns] += nn(exact.astype(bf16), dstacked)

        return products, rest

    return [task(*unit) for unit in short_units(rows)]


def project_to(tokens, low, weight, extra, scale=None):
    value = nn(tokens, weight)
    if extra is not None:
        value = value + nn(low, extra)
    value = value.astype(bf16)
    return value if scale is None else value * jnp.asarray(scale, bf16)


def project_task(tokens, low, weight, extra, put, scale=None, before=None):
    def products():
        if before is not None:
            before()
        value = nn(tokens[...], weight() if callable(weight) else weight[...])
        return value if extra is None else value + nn(low(), extra[...])

    def rest(value):
        value = value.astype(bf16)
        put(value if scale is None else value * jnp.asarray(scale, bf16))

    return products, rest


def setter(target):
    def put(value):
        target[...] = value

    return put


def dense_tasks(tokens, context, weights, gains, hidden, out, kept=None, ready=None):
    out_weight, inner_weight, outer_weight = weights
    attention_gain, output_gain = gains
    rows, width = tokens.shape
    count = 2 if kept else 4
    halves = [slice(i * rows // count, (i + 1) * rows // count) for i in range(count)]
    chunks = [slice(start, start + CHUNK) for start in range(0, hidden.shape[1], CHUNK)]
    ready = ready or {}
    unit, inverse = (kept["unit"], kept["inverse"]) if kept else (ready["unit"], None)
    low = out

    def wait(name):
        if name in ready:
            ready.pop(name)()

    def attend_out(r):
        def products():
            wait("out")
            return nn(context[r, :], out_weight[...])

        def rest(value):
            scaled, factor = normalize(tokens[r, :].astype(f32) + value)
            if kept:
                inverse[r, :] = factor
                unit[r, :] = scaled
                low[r, :] = (scaled * attention_gain).astype(bf16)
            else:
                middle = scaled * attention_gain
                unit[r, :] = middle
                low[r, :] = middle.astype(bf16)

        return products, rest

    def inner_part(r, columns):
        def products():
            wait(("inner", columns.start))
            return nn(low[r, :], inner_weight[:, columns])

        def rest(inner):
            phi = 0.5 + 0.5 * lax.erf(inner * 0.7071067811865476)
            hidden[r, columns] = (inner * phi).astype(bf16)
            if kept:
                kept["slope"][r, columns] = phi + inner * (
                    jnp.exp(-0.5 * inner * inner) * 0.3989422804014327
                )

        return products, rest

    def outer_part(r):
        def products():
            wait("outer")
            return nn(hidden[r, :], outer_weight[...])

        def rest(value):
            middle = unit[r, :] * attention_gain if kept else unit[r, :]
            scaled, factor = normalize(middle + value)
            out[r, :] = (scaled * output_gain).astype(bf16)
            if kept:
                dsecond = normalize_back(kept["cotangent"][r, :] * output_gain, scaled, factor)
                kept["dfirst"][r, :] = dsecond
                kept["dlow"][r, :] = dsecond.astype(bf16)

        return products, rest

    def outer_back(r, columns):
        def products():
            return nt(kept["dlow"][r, :], outer_weight[columns, :])

        def rest(dhidden):
            hidden[r, columns] = (dhidden * kept["slope"][r, columns]).astype(bf16)

        return products, rest

    def inner_back(r):
        def products():
            wait("written")
            return nt(hidden[r, :], inner_weight[...])

        def rest(value):
            dmiddle = kept["dfirst"][r, :] + value
            dfirst = normalize_back(dmiddle * attention_gain, unit[r, :], inverse[r, :])
            kept["dfirst"][r, :] = dfirst
            kept["dlow"][r, :] = dfirst.astype(bf16)

        return products, rest

    def attend_back(r):
        def products():
            return nt(kept["dlow"][r, :], out_weight[...])

        def rest(value):
            kept["dcontext"][r, :] = value.astype(bf16)

        return products, rest

    tasks = [attend_out(r) for r in halves]
    tasks += [inner_part(r, columns) for r in halves for columns in chunks]
    tasks += [outer_part(r) for r in halves]
    if kept:
        tasks += [outer_back(r, columns) for r in halves for columns in chunks]
        tasks += [inner_back(r) for r in halves]
        tasks += [attend_back(r) for r in halves]
    return tasks


class Copies:
    def __init__(self, semaphores):
        self.semaphores = semaphores
        self.count = 0

    def start(self, source, target):
        copy = pltpu.make_async_copy(source, target, self.semaphores.at[self.count])
        self.count += 1
        copy.start()
        return copy


def start_all(copies, pairs):
    return [copies.start(source, target) for source, target in pairs]


def short_kernel(
    lengths, query_down, query_up, value_down, value_up, attention_gain_in, output_gain_in,
    tokens_in, cotangent_in, query_in, key_in, value_in, out_in, inner_in, outer_in,
    out_out, grad_out, up_out, factors_out,
    tokens, cotangent, query_weight, key_weight, value_weight, out_weight, inner_weight, outer_weight,
    down, query_rows, value_rows, bias, queries, keys, values, context, shares,
    unit, inverse, dfirst, slope, hidden, out, dlow, semaphores,
):
    rows, width = tokens.shape
    copies = Copies(semaphores)
    waits = start_all(
        copies,
        (
            (tokens_in, tokens), (query_in, query_weight), (key_in, key_weight), (value_in, value_weight),
        ),
    )
    fill_factors(query_down, value_down, query_up, value_up, down, query_rows, value_rows)
    segment_bias(lengths, bias, rows)
    gains = (attention_gain_in[...].reshape(1, width), output_gain_in[...].reshape(1, width))
    waits[0].wait()
    low = nt(tokens[...], down[...]).astype(bf16)
    dense = (out_weight, inner_weight, outer_weight)
    dcontext = context
    kept = dict(
        unit=unit, inverse=inverse, dfirst=dfirst, slope=slope, dlow=dlow, cotangent=cotangent, dcontext=dcontext,
    )
    dqueries = hidden.at[:, 0:width]
    dkeys, dvalues = slope.at[:, 0:width], slope.at[:, width : 2 * width]
    sent = []

    def dense_copies():
        waits[2].wait()
        waits[3].wait()
        waits.extend(
            start_all(
                copies,
                (
                    (out_in, out_weight), (inner_in, inner_weight), (outer_in, outer_weight),
                    (cotangent_in, cotangent),
                ),
            )
        )

    def dense_waits():
        for wait in waits[4:]:
            wait.wait()

    def write_out():
        sent.append(copies.start(out, out_out))
        for packed, room in factor_pairs(factors_out, (down, query_rows, value_rows)):
            sent.append(copies.start(room, packed))

    def finish(r):
        def products():
            dquery, dkey, dvalue = dqueries[r, :], dkeys[r, :].astype(bf16), dvalues[r, :].astype(bf16)
            dlatent = (nt(dquery, query_rows[...]) + nt(dvalue, value_rows[...])).astype(bf16)
            return (
                nt(dquery, query_weight[...])
                + nt(dkey, key_weight[...])
                + nt(dvalue, value_weight[...])
                + nn(dlatent, down[...])
            )

        def rest(value):
            cotangent[r, :] = dfirst[r, :] + value
            sent.append(copies.start(cotangent.at[r, :], grad_out.at[r, :]))

        return products, rest

    run_tasks(
        [
            project_task(
                tokens, lambda: low, query_weight, query_rows, setter(queries), head_scale, waits[1].wait
            ),
            project_task(tokens, None, key_weight, None, setter(keys), None, dense_copies),
            project_task(tokens, lambda: low, value_weight, value_rows, setter(values)),
            *short_attention_tasks(queries, keys, values, bias, context, shares, rows),
            *dense_tasks(
                tokens, context, dense, gains, hidden, out, kept, dict(out=dense_waits, written=write_out)
            ),
            *short_attention_back_tasks(
                queries, keys, values, dcontext, shares, dqueries, dkeys, dvalues, rows
            ),
            finish(slice(0, rows // 2)),
            finish(slice(rows // 2, rows)),
        ]
    )
    low = nt(tokens[...], down[...]).astype(bf16)
    dquery, dvalue = dqueries[...], dvalues[...].astype(bf16)
    up_out[0:RANK, :] = adapter_scale * tn(low, dquery)[0:RANK, :]
    up_out[RANK : 2 * RANK, :] = adapter_scale * tn(low, dvalue)[RANK : 2 * RANK, :]
    for copy in sent:
        copy.wait()


def long_kernel(
    lengths_in, factors_in, attention_gain_in, output_gain_in, short_up_in,
    tokens_in, far_in, cotangent_in, query_in, key_in, value_in, out_in, inner_in, outer_in,
    out_out, near_out, far_out, up_out,
    tokens, far, cotangent, query_weight, key_weight, value_weight, out_weight, inner_weight, outer_weight,
    down, query_rows, value_rows, queries, keys, values, context, shares,
    unit, inverse, dfirst, slope, hidden, out, dlow, low, lengths, gain, gain_out, short_up, semaphores,
):
    rows, width = tokens.shape
    items = lengths.shape[0]
    half = rows // items
    copies = Copies(semaphores)
    small = start_all(
        copies,
        (
            *factor_pairs(factors_in, (down, query_rows, value_rows)), (lengths_in, lengths),
            (attention_gain_in, gain), (output_gain_in, gain_out), (short_up_in, short_up),
        ),
    )
    waits = start_all(
        copies,
        (
            (tokens_in, tokens), (query_in, query_weight), (far_in, far), (key_in, key_weight),
            (value_in, value_weight),
        ),
    )
    clear_tails((down, query_rows, value_rows))
    place = lax.axis_index("blk")

    def part(item, which):
        start = 2 * item * half + (place if which == 0 else 1 - place) * half
        return pl.ds(pl.multiple_of(start, half), half)

    def put(target, which, value):
        for item in range(items):
            target[part(item, which), :] = value[item * half : (item + 1) * half]

    for wait in small:
        wait.wait()
    gains = (gain[...].reshape(1, width), gain_out[...].reshape(1, width))
    waits[0].wait()
    low[0:rows, :] = nt(tokens[...], down[...]).astype(bf16)
    waits[1].wait()
    queries[...] = project_to(tokens[...], low[0:rows, :], query_weight[...], query_rows[...], head_scale)
    for wait in waits[2:5]:
        wait.wait()
    waits += start_all(
        copies,
        (
            (out_in, out_weight), (inner_in, inner_weight), (outer_in, outer_weight), (cotangent_in, cotangent),
        ),
    )
    low[rows:, :] = nt(far[...], down[...]).astype(bf16)
    put(keys, 0, project_to(tokens[...], None, key_weight[...], None))
    put(keys, 1, project_to(far[...], None, key_weight[...], None))
    put(values, 0, project_to(tokens[...], low[0:rows, :], value_weight[...], value_rows[...]))
    put(values, 1, project_to(far[...], low[rows:, :], value_weight[...], value_rows[...]))

    units = [
        (
            item * GROUPS + index, item, slice(index * WIDE, (index + 1) * WIDE),
            slice(item * half, (item + 1) * half), slice(2 * item * half, 2 * (item + 1) * half),
        )
        for item in range(items)
        for index in range(GROUPS)
    ]
    place_in_half = lax.broadcasted_iota(jnp.int32, (half, LANES), 0) + half
    masks = []
    for item in range(items):
        mask = jnp.where(place_in_half < lengths[item], 0.0, masked_score)
        masks.append(jnp.concatenate([mask] * (STACK * half // LANES), axis=1))

    def forward(number, item, columns, own, joined):
        def products():
            return nt(keys[joined, columns], stack_heads(queries[own, columns]))

        def rest(scores):
            scores = jnp.concatenate([scores[0:half], scores[half:] + masks[item]], axis=0)
            exact = softmax_columns(scores).astype(bf16)
            shares[number] = exact
            turned = jnp.swapaxes(values[joined, columns], 0, 1)
            context[own, columns] = join_heads(turned, exact, half).astype(bf16)

        return products, rest

    run_tasks([forward(*unit_) for unit_ in units])
    for wait in waits[5:]:
        wait.wait()
    dense = (out_weight, inner_weight, outer_weight)
    dcontext = context
    kept = dict(
        unit=unit, inverse=inverse, dfirst=dfirst, slope=slope, dlow=dlow, cotangent=cotangent, dcontext=dcontext,
    )
    run_tasks(dense_tasks(tokens, context, dense, gains, hidden, out, kept))
    sent = [copies.start(out, out_out)]
    dqueries = dlow
    dkeys = hidden.at[:, 0 : 2 * width]
    dvalues = hidden.at[:, 2 * width : 4 * width]

    def backward(number, item, columns, own, joined):
        def products():
            dstacked = stack_heads(dcontext[own, columns])
            return dstacked, nt(values[joined, columns], dstacked)

        def rest(value):
            dstacked, dshares = value
            exact = shares[number].astype(f32)
            inner = jnp.sum(exact * dshares, axis=0, keepdims=True)
            dscores = (exact * (dshares - inner)).astype(bf16)
            turned = jnp.swapaxes(keys[joined, columns], 0, 1)
            dqueries[own, columns] = (join_heads(turned, dscores, half) * head_scale).astype(bf16)
            dkey = nn(dscores, stack_heads(queries[own, columns])).astype(bf16)
            dvalue = nn(shares[number], dstacked).astype(bf16)
            for which in range(2):
                rows_ = slice(which * half, (which + 1) * half)
                target = slice(which * width + columns.start, which * width + columns.stop)
                dkeys[own, target] = dkey[rows_]
                dvalues[own, target] = dvalue[rows_]

        return products, rest

    run_tasks([backward(*unit_) for unit_ in units])

    def back_part(which):
        start = pl.multiple_of((place if which == 0 else 1 - place) * width, LANES)
        return dkeys[:, pl.ds(start, width)], dvalues[:, pl.ds(start, width)]

    dkey, dvalue = back_part(1)
    dlatent = nt(dvalue, value_rows[...]).astype(bf16)
    unit[...] = nt(dkey, key_weight[...]) + nt(dvalue, value_weight[...]) + nn(dlatent, down[...])
    sent.append(copies.start(unit, far_out))
    up = tn(low[rows:, :], dvalue)[RANK : 2 * RANK, :]
    dquery = dqueries[...]
    dkey, dvalue = back_part(0)
    dlatent = (nt(dquery, query_rows[...]) + nt(dvalue, value_rows[...])).astype(bf16)
    for r in (slice(0, rows // 2), slice(rows // 2, rows)):
        cotangent[r, :] = (
            dfirst[r, :]
            + nt(dquery[r], query_weight[...])
            + nt(dkey[r], key_weight[...])
            + nt(dvalue[r], value_weight[...])
            + nn(dlatent[r], down[...])
        )
        sent.append(copies.start(cotangent.at[r, :], near_out.at[r, :]))
    up = up + tn(low[0:rows, :], dvalue)[RANK : 2 * RANK, :]
    up_out[0:RANK, :] = adapter_scale * tn(low[0:rows, :], dquery)[0:RANK, :] + short_up[0:RANK, :]
    up_out[RANK : 2 * RANK, :] = adapter_scale * up + short_up[RANK : 2 * RANK, :]
    for copy in sent:
        copy.wait()


def eval_attention_kernel(
    lengths_in, factors_in, after,
    tokens_in, query_in, key_in, value_in,
    context,
    tokens, query_weight, key_weight, value_weight,
    down, query_rows, value_rows, bias, queries, keys, values, lengths, semaphores,
):
    rows, width = tokens.shape
    copies = Copies(semaphores)
    small = start_all(
        copies, ((lengths_in, lengths), *factor_pairs(factors_in, (down, query_rows, value_rows)))
    )
    waits = start_all(
        copies,
        (
            (tokens_in, tokens), (key_in, key_weight), (query_in, query_weight), (value_in, value_weight),
        ),
    )
    clear_tails((down, query_rows, value_rows))
    for wait in small:
        wait.wait()
    segment_bias(lengths, bias, rows)
    waits[0].wait()

    def merged(weight, extra):
        return lambda: (weight[...].astype(f32) + tn(down[...], extra[...])).astype(bf16)

    run_tasks(
        [
            project_task(tokens, None, key_weight, None, setter(keys), None, waits[1].wait),
            project_task(
                tokens, None, merged(query_weight, query_rows), None, setter(queries), head_scale, waits[2].wait
            ),
            project_task(
                tokens, None, merged(value_weight, value_rows), None, setter(values), None, waits[3].wait
            ),
            *short_attention_tasks(queries, keys, values, bias, context, None, rows),
        ]
    )


def eval_dense_kernel(
    attention_gain_in, output_gain_in, after,
    tokens_in, context_in, out_in, inner_in, outer_in, near_in, far_in,
    out_out, grad_out,
    tokens, context, out_weight, inner_weight, outer_weight, near, far, unit, hidden, gain, gain_out, semaphores,
):
    width = tokens.shape[1]
    copies = Copies(semaphores)
    first = start_all(
        copies,
        (
            (attention_gain_in, gain), (output_gain_in, gain_out),
            (context_in, context), (out_in, out_weight), (tokens_in, tokens),
        ),
    )
    inner = {}
    for start in range(0, hidden.shape[1], CHUNK):
        columns = slice(start, start + CHUNK)
        inner[start] = copies.start(inner_in.at[:, columns], inner_weight.at[:, columns])
    outer, *last = start_all(copies, ((outer_in, outer_weight), (near_in, near), (far_in, far)))
    ready = {("inner", start): copy.wait for start, copy in inner.items()}
    ready["outer"] = outer.wait
    ready["unit"] = unit
    for wait in first:
        wait.wait()
    gains = (gain[...].reshape(1, width), gain_out[...].reshape(1, width))
    dense = (out_weight, inner_weight, outer_weight)
    tasks = dense_tasks(tokens, context, dense, gains, hidden, out_out, None, ready)
    sent = []

    def gradient_waits():
        for wait in last:
            wait.wait()

    def gradient_sum(unused):
        near[...] = near[...] + far[...]
        sent.append(copies.start(near, grad_out))

    tasks.insert(len(tasks) - 4, (gradient_waits, gradient_sum))
    run_tasks(tasks)
    sent[0].wait()


IN_VMEM = pl.BlockSpec(memory_space=pltpu.VMEM)
IN_SMEM = pl.BlockSpec(memory_space=pltpu.SMEM)
ANYWHERE = pl.BlockSpec(memory_space=pl.ANY)
FACTORS = [IN_VMEM] * 4


def kernel_call(kernel, in_specs, out_specs, out_shape, scratch, copies, flops, moved, name):
    return pl.pallas_call(
        kernel,
        in_specs=in_specs,
        out_specs=out_specs,
        out_shape=out_shape,
        scratch_shapes=[*scratch, pltpu.SemaphoreType.DMA((copies,))],
        compiler_params=pltpu.CompilerParams(vmem_limit_bytes=VMEM_LIMIT),
        cost_estimate=pl.CostEstimate(flops=int(flops), bytes_accessed=int(moved), transcendentals=0),
        name=name,
    )


def shape(dims, kind):
    return jax.ShapeDtypeStruct(dims, kind)


def vm(dims, kind):
    return pltpu.VMEM(dims, kind)


def weight_room(width, wide):
    square = vm((width, width), bf16)
    return [square, square, square, square, vm((width, wide), bf16), vm((wide, width), bf16)]


def factor_room(width):
    return [vm((LANES, width), bf16)] * 3


def kept_room(rows, width, wide):
    return [
        vm((rows, width), f32), vm((rows, 1), f32), vm((rows, width), f32),
        vm((rows, wide), f32), vm((rows, wide), bf16), vm((rows, width), bf16), vm((rows, width), bf16),
    ]


def partner(value, axis, mask):
    count = lax.axis_size(axis)
    return lax.ppermute(value, axis, [(i, i ^ mask) for i in range(count)])


def quad_parts(value, axis, bit):
    masks = [mask * bit for mask in (1, 2, 3) if mask * bit < lax.axis_size(axis)]
    return [value, *[partner(value, axis, mask) for mask in masks]]


def add_up(parts):
    return functools.reduce(lambda a, b: a + b, parts)


def run_short(lengths, factors, gains, tokens, cotangent, weights):
    rows, width = tokens.shape
    wide = weights[4].shape[1]
    blocks = rows // BLOCK
    return kernel_call(
        short_kernel,
        [IN_SMEM, *FACTORS, IN_VMEM, IN_VMEM, *[ANYWHERE] * 8],
        [ANYWHERE, ANYWHERE, IN_VMEM, ANYWHERE],
        [
            shape((rows, width), bf16), shape((rows, width), f32), shape((2 * RANK, width), f32),
            shape((6 * RANK, width), bf16),
        ],
        [
            vm((rows, width), bf16), vm((rows, width), f32), *weight_room(width, wide), *factor_room(width),
            vm((blocks, WINDOW, BLOCK), f32), *[vm((rows, width), bf16)] * 4,
            vm((GROUPS, blocks, WINDOW, STACK * BLOCK), f32), *kept_room(rows, width, wide),
        ],
        16, 20e9, 25e6, "short_step",
    )(lengths, *factors, *gains, tokens, cotangent, *weights)


def run_long(lengths, factors, gains, short_up, tokens, far, cotangent, weights):
    rows, width = tokens.shape
    wide = weights[4].shape[1]
    items = lengths.shape[0]
    half = rows // items
    return kernel_call(
        long_kernel,
        [ANYWHERE] * 14,
        [ANYWHERE, ANYWHERE, ANYWHERE, IN_VMEM],
        [
            shape((rows, width), bf16), shape((rows, width), f32), shape((rows, width), f32),
            shape((2 * RANK, width), f32),
        ],
        [
            vm((rows, width), bf16), vm((rows, width), bf16), vm((rows, width), f32),
            *weight_room(width, wide), *factor_room(width), vm((rows, width), bf16),
            *[vm((2 * rows, width), bf16)] * 2, vm((rows, width), bf16),
            vm((items * GROUPS, 2 * half, STACK * half), bf16), *kept_room(rows, width, wide),
            vm((2 * rows, LANES), bf16), pltpu.SMEM((items,), jnp.int32), vm((width,), f32), vm((width,), f32),
            vm((2 * RANK, width), f32),
        ],
        24, 22e9, 30e6, "long_step",
    )(lengths, factors, *gains, short_up, tokens, far, cotangent, *weights)


def run_eval_attention(lengths, factors, after, tokens, weights):
    rows, width = tokens.shape
    blocks = rows // BLOCK
    return kernel_call(
        eval_attention_kernel,
        [ANYWHERE] * 7,
        IN_VMEM,
        shape((rows, width), bf16),
        [
            vm((rows, width), bf16), *[vm((width, width), bf16)] * 3, *factor_room(width),
            vm((blocks, WINDOW, BLOCK), f32), *[vm((rows, width), bf16)] * 3,
            pltpu.SMEM(lengths.shape, jnp.int32),
        ],
        8, 4e9, 6e6, "eval_attention",
    )(lengths, factors, after, tokens, *weights[0:3])


def run_eval_dense(gains, after, tokens, context, weights, near, far):
    rows, width = tokens.shape
    wide = weights[4].shape[1]
    return kernel_call(
        eval_dense_kernel,
        [ANYWHERE] * 10,
        [IN_VMEM, ANYWHERE],
        [shape((rows, width), bf16), shape((rows, width), f32)],
        [
            vm((rows, width), bf16), vm((rows, width), bf16), *weight_room(width, wide)[3:],
            vm((rows, width), f32), vm((rows, width), f32), vm((rows, width), f32), vm((rows, wide), bf16),
            vm((width,), f32), vm((width,), f32),
        ],
        12, 6e9, 18e6, "eval_dense",
    )(*gains, after, tokens, context, *weights[3:], near, far)


def body(
    short_tokens, short_lengths, long_tokens, long_lengths, eval_tokens, eval_lengths,
    query_matrix, key_weight, value_matrix, out_weight, inner_weight, outer_weight,
    query_down_factor, query_up_factor, value_down_factor, value_up_factor,
    attention_gain, output_gain, cot_short, cot_long,
):
    items, half, width = long_tokens.shape
    factors = (query_down_factor.T, query_up_factor, value_down_factor.T, value_up_factor)
    gains = (attention_gain, output_gain)
    weights = (query_matrix, key_weight, value_matrix, out_weight, inner_weight, outer_weight)

    long_flat = long_tokens.reshape(items * half, width)
    far_flat = partner(long_flat, "blk", 1)
    short_out, short_grad, short_up, packed = run_short(
        short_lengths, factors, gains, short_tokens, cot_short, weights
    )
    long_out, near_grad, far_grad, up = run_long(
        long_lengths, packed, gains, short_up, long_flat, far_flat,
        cot_long.reshape(items * half, width), weights,
    )
    up = up + partner(up, "blk", 1)
    up, far_grad = lax.optimization_barrier((up, far_grad))
    arrived = partner(far_grad, "blk", 1)

    stages = []
    bit = 1
    while bit < lax.axis_size("dp"):
        stages.append(bit)
        bit *= 4
    parts = quad_parts(up, "dp", stages[0])
    context = run_eval_attention(eval_lengths, packed, up, eval_tokens, weights)
    context, arrived, *parts = lax.optimization_barrier((context, arrived, *parts))
    first_sum = add_up(parts)
    for bit in stages[1:]:
        parts = quad_parts(add_up(parts), "dp", bit)
    eval_out, long_grad = run_eval_dense(
        gains, first_sum, eval_tokens, context, weights, near_grad, arrived
    )
    eval_out, *parts = lax.optimization_barrier((eval_out, *parts))
    query_up_grad = add_up([part[0:RANK] for part in parts])
    value_up_grad = add_up([part[RANK:] for part in parts])

    return (
        short_out,
        long_out.reshape(items, half, width),
        short_grad,
        long_grad.reshape(items, half, width),
        query_up_grad,
        value_up_grad,
        eval_out,
    )


def solution(mesh):
    rows = P(("dp", "blk"), None)
    items = P("dp", "blk", None)
    return jax.shard_map(
        body,
        mesh=mesh,
        in_specs=(
            rows, rows, items, P("dp"), rows, rows, *[P()] * 12, rows, items,
        ),
        out_specs=(rows, items, rows, items, P(), P(), rows),
        check_vma=False,
    )
```

```python
import functools

import jax
import jax.numpy as jnp
from jax import lax
from jax.experimental import pallas as pl
from jax.experimental.pallas import tpu as pltpu
from jax.sharding import PartitionSpec as P

HEADS = 12
HEAD = 64
STACK = 4
WIDE = STACK * HEAD
GROUPS = HEADS // STACK
BLOCK = 128
WINDOW = 256
REACH = 64
LANES = 128
RANK = 8
VMEM_LIMIT = 62 * 2**20
CHUNK = 1024

adapter_scale = 2.0
norm_eps = 1e-05
masked_score = -1000000000.0
head_scale = HEAD ** (-0.5)

bf16 = jnp.bfloat16
f32 = jnp.float32


def nn(left, right):
    return jnp.dot(left, right, preferred_element_type=f32)


def nt(left, right):
    return lax.dot_general(left, right, (((1,), (1,)), ((), ())), preferred_element_type=f32)


def tn(left, right):
    return lax.dot_general(left, right, (((0,), (0,)), ((), ())), preferred_element_type=f32)


def fill_factors(query_down, value_down, query_up, value_up, down, query_rows, value_rows):
    width = down.shape[1]
    blank = jnp.zeros((RANK, width), f32)
    rest = jnp.zeros((LANES - 2 * RANK, width), bf16)
    query_two = adapter_scale * query_up[...].astype(f32)
    value_two = adapter_scale * value_up[...].astype(f32)
    both = [query_down[...].astype(f32), value_down[...].astype(f32)]
    for target, parts in (
        (down, both), (query_rows, [query_two, blank]), (value_rows, [blank, value_two]),
    ):
        target[0 : 2 * RANK, :] = jnp.concatenate(parts, axis=0).astype(bf16)
        target[2 * RANK :, :] = rest


def factor_pairs(factors, rooms):
    size = 2 * RANK
    return [
        (factors.at[i * size : (i + 1) * size, :], room.at[0:size, :]) for i, room in enumerate(rooms)
    ]


def clear_tails(rooms):
    for room in rooms:
        room[2 * RANK :, :] = jnp.zeros((LANES - 2 * RANK, room.shape[1]), bf16)


def head_masks():
    lane = lax.broadcasted_iota(jnp.int32, (1, WIDE), 1)
    return [(lane >= h * HEAD) & (lane < (h + 1) * HEAD) for h in range(STACK)]


def stack_heads(value):
    zero = jnp.zeros_like(value)
    return jnp.concatenate([jnp.where(mask, value, zero) for mask in head_masks()], axis=0)


def unstack_heads(value):
    rows = value.shape[0] // STACK
    lane = lax.broadcasted_iota(jnp.int32, (1, LANES), 1)
    low = lane < HEAD
    parts = []
    for pair in range(STACK // 2):
        columns = slice(pair * LANES, (pair + 1) * LANES)
        first = value[2 * pair * rows : (2 * pair + 1) * rows, columns]
        second = value[(2 * pair + 1) * rows : (2 * pair + 2) * rows, columns]
        parts.append(jnp.where(low, first, second))
    return jnp.concatenate(parts, axis=1)


def join_heads(turned, right, count):
    parts = [
        nn(turned[h * HEAD : (h + 1) * HEAD], right[:, h * count : (h + 1) * count]) for h in range(STACK)
    ]
    return jnp.swapaxes(jnp.concatenate(parts, axis=0), 0, 1)


def normalize(value):
    centre = value - jnp.mean(value, axis=-1, keepdims=True)
    inverse = lax.rsqrt(jnp.mean(centre * centre, axis=-1, keepdims=True) + norm_eps)
    return centre * inverse, inverse


def normalize_back(grad, unit, inverse):
    return inverse * (
        grad
        - jnp.mean(grad, axis=-1, keepdims=True)
        - unit * jnp.mean(grad * unit, axis=-1, keepdims=True)
    )


def segment_bias(lengths, bias, rows):
    key_place = lax.broadcasted_iota(jnp.int32, (rows, LANES), 0)
    query_place = lax.broadcasted_iota(jnp.int32, (8, rows), 1)
    key_segment = jnp.zeros((rows, LANES), jnp.int32)
    query_segment = jnp.zeros((8, rows), jnp.int32)
    end = jnp.int32(0)
    for item in range(lengths.shape[1]):
        end = end + lengths[0, item]
        key_segment = key_segment + (key_place >= end).astype(jnp.int32)
        query_segment = query_segment + (query_place >= end).astype(jnp.int32)
    for block in range(rows // BLOCK):
        start = window_start(block, rows)
        same = (
            key_segment[start : start + WINDOW, :]
            == query_segment[0:1, block * BLOCK : (block + 1) * BLOCK]
        )
        bias[block] = jnp.where(same, 0.0, masked_score)


def window_start(block, rows):
    return min(max(block * BLOCK - REACH, 0), rows - WINDOW)


def run_tasks(tasks):
    rest = None
    for products, after in tasks:
        value = products()
        if rest is not None:
            rest()
        rest = functools.partial(after, value)
    rest()


def softmax_columns(scores):
    peak = jnp.max(scores, axis=0, keepdims=True)
    powers = jnp.exp(scores - peak)
    return powers * (1.0 / jnp.sum(powers, axis=0, keepdims=True))


def short_units(rows):
    for block in range(rows // BLOCK):
        for index in range(GROUPS):
            start = window_start(block, rows)
            yield (
                index, block, slice(index * WIDE, (index + 1) * WIDE),
                slice(block * BLOCK, (block + 1) * BLOCK), slice(start, start + WINDOW),
            )


def short_attention_tasks(queries, keys, values, bias, context, shares, rows):
    def task(index, block, columns, own, window):
        def products():
            return nt(keys[window, columns], stack_heads(queries[own, columns]))

        def rest(scores):
            exact = softmax_columns(scores + jnp.concatenate([bias[block]] * STACK, axis=1))
            if shares is not None:
                shares[index, block] = exact
            mixed = tn(exact.astype(bf16), values[window, columns])
            context[own, columns] = unstack_heads(mixed).astype(bf16)

        return products, rest

    return [task(*unit) for unit in short_units(rows)]


def short_attention_back_tasks(queries, keys, values, dcontext, shares, dqueries, dkeys, dvalues, rows):
    def task(index, block, columns, own, window):
        def products():
            if index == 0 and block == 0:
                dkeys[...] = jnp.zeros_like(dkeys)
                dvalues[...] = jnp.zeros_like(dvalues)
            dstacked = stack_heads(dcontext[own, columns])
            return dstacked, nt(values[window, columns], dstacked)

        def rest(value):
            dstacked, dshares = value
            exact = shares[index, block]
            inner = jnp.sum(exact * dshares, axis=0, keepdims=True)
            dscores = (exact * (dshares - inner)).astype(bf16)
            mixed = tn(dscores, keys[window, columns])
            dqueries[own, columns] = (unstack_heads(mixed) * head_scale).astype(bf16)
            dkeys[window, columns] += nn(dscores, stack_heads(queries[own, columns]))
            dvalues[window, columns] += nn(exact.astype(bf16), dstacked)

        return products, rest

    return [task(*unit) for unit in short_units(rows)]


def project_to(tokens, low, weight, extra, scale=None):
    value = nn(tokens, weight)
    if extra is not None:
        value = value + nn(low, extra)
    value = value.astype(bf16)
    return value if scale is None else value * jnp.asarray(scale, bf16)


def project_task(tokens, low, weight, extra, put, scale=None, before=None):
    def products():
        if before is not None:
            before()
        value = nn(tokens[...], weight() if callable(weight) else weight[...])
        return value if extra is None else value + nn(low(), extra[...])

    def rest(value):
        value = value.astype(bf16)
        put(value if scale is None else value * jnp.asarray(scale, bf16))

    return products, rest


def setter(target):
    def put(value):
        target[...] = value

    return put


def dense_tasks(tokens, context, weights, gains, hidden, out, kept=None, ready=None):
    out_weight, inner_weight, outer_weight = weights
    attention_gain, output_gain = gains
    rows, width = tokens.shape
    count = 2 if kept else 4
    halves = [slice(i * rows // count, (i + 1) * rows // count) for i in range(count)]
    chunks = [slice(start, start + CHUNK) for start in range(0, hidden.shape[1], CHUNK)]
    ready = ready or {}
    unit, inverse = (kept["unit"], kept["inverse"]) if kept else (ready["unit"], None)
    low = out

    def wait(name):
        if name in ready:
            ready.pop(name)()

    def attend_out(r):
        def products():
            wait("out")
            return nn(context[r, :], out_weight[...])

        def rest(value):
            scaled, factor = normalize(tokens[r, :].astype(f32) + value)
            if kept:
                inverse[r, :] = factor
                unit[r, :] = scaled
                low[r, :] = (scaled * attention_gain).astype(bf16)
            else:
                middle = scaled * attention_gain
                unit[r, :] = middle
                low[r, :] = middle.astype(bf16)

        return products, rest

    def inner_part(r, columns):
        def products():
            wait(("inner", columns.start))
            return nn(low[r, :], inner_weight[:, columns])

        def rest(inner):
            phi = 0.5 + 0.5 * lax.erf(inner * 0.7071067811865476)
            hidden[r, columns] = (inner * phi).astype(bf16)
            if kept:
                kept["slope"][r, columns] = phi + inner * (
                    jnp.exp(-0.5 * inner * inner) * 0.3989422804014327
                )

        return products, rest

    def outer_part(r):
        def products():
            wait("outer")
            return nn(hidden[r, :], outer_weight[...])

        def rest(value):
            middle = unit[r, :] * attention_gain if kept else unit[r, :]
            scaled, factor = normalize(middle + value)
            out[r, :] = (scaled * output_gain).astype(bf16)
            if kept:
                dsecond = normalize_back(kept["cotangent"][r, :] * output_gain, scaled, factor)
                kept["dfirst"][r, :] = dsecond
                kept["dlow"][r, :] = dsecond.astype(bf16)

        return products, rest

    def outer_back(r, columns):
        def products():
            return nt(kept["dlow"][r, :], outer_weight[columns, :])

        def rest(dhidden):
            hidden[r, columns] = (dhidden * kept["slope"][r, columns]).astype(bf16)

        return products, rest

    def inner_back(r):
        def products():
            wait("written")
            return nt(hidden[r, :], inner_weight[...])

        def rest(value):
            dmiddle = kept["dfirst"][r, :] + value
            dfirst = normalize_back(dmiddle * attention_gain, unit[r, :], inverse[r, :])
            kept["dfirst"][r, :] = dfirst
            kept["dlow"][r, :] = dfirst.astype(bf16)

        return products, rest

    def attend_back(r):
        def products():
            return nt(kept["dlow"][r, :], out_weight[...])

        def rest(value):
            kept["dcontext"][r, :] = value.astype(bf16)

        return products, rest

    tasks = [attend_out(r) for r in halves]
    tasks += [inner_part(r, columns) for r in halves for columns in chunks]
    tasks += [outer_part(r) for r in halves]
    if kept:
        tasks += [outer_back(r, columns) for r in halves for columns in chunks]
        tasks += [inner_back(r) for r in halves]
        tasks += [attend_back(r) for r in halves]
    return tasks


class Copies:
    def __init__(self, semaphores):
        self.semaphores = semaphores
        self.count = 0

    def start(self, source, target):
        copy = pltpu.make_async_copy(source, target, self.semaphores.at[self.count])
        self.count += 1
        copy.start()
        return copy


def start_all(copies, pairs):
    return [copies.start(source, target) for source, target in pairs]


def short_kernel(
    lengths, query_down, query_up, value_down, value_up, attention_gain_in, output_gain_in,
    tokens_in, cotangent_in, query_in, key_in, value_in, out_in, inner_in, outer_in,
    out_out, grad_out, up_out, factors_out,
    tokens, cotangent, query_weight, key_weight, value_weight, out_weight, inner_weight, outer_weight,
    down, query_rows, value_rows, bias, queries, keys, values, context, shares,
    unit, inverse, dfirst, slope, hidden, out, dlow, semaphores,
):
    rows, width = tokens.shape
    copies = Copies(semaphores)
    waits = start_all(
        copies,
        (
            (tokens_in, tokens), (query_in, query_weight), (key_in, key_weight), (value_in, value_weight),
        ),
    )
    fill_factors(query_down, value_down, query_up, value_up, down, query_rows, value_rows)
    segment_bias(lengths, bias, rows)
    gains = (attention_gain_in[...].reshape(1, width), output_gain_in[...].reshape(1, width))
    waits[0].wait()
    low = nt(tokens[...], down[...]).astype(bf16)
    dense = (out_weight, inner_weight, outer_weight)
    dcontext = context
    kept = dict(
        unit=unit, inverse=inverse, dfirst=dfirst, slope=slope, dlow=dlow, cotangent=cotangent, dcontext=dcontext,
    )
    dqueries = hidden.at[:, 0:width]
    dkeys, dvalues = slope.at[:, 0:width], slope.at[:, width : 2 * width]
    sent = []

    def dense_copies():
        waits[2].wait()
        waits[3].wait()
        waits.extend(
            start_all(
                copies,
                (
                    (out_in, out_weight), (inner_in, inner_weight), (outer_in, outer_weight),
                    (cotangent_in, cotangent),
                ),
            )
        )

    def dense_waits():
        for wait in waits[4:]:
            wait.wait()

    def write_out():
        sent.append(copies.start(out, out_out))
        for packed, room in factor_pairs(factors_out, (down, query_rows, value_rows)):
            sent.append(copies.start(room, packed))

    def finish(r):
        def products():
            dquery, dkey, dvalue = dqueries[r, :], dkeys[r, :].astype(bf16), dvalues[r, :].astype(bf16)
            dlatent = (nt(dquery, query_rows[...]) + nt(dvalue, value_rows[...])).astype(bf16)
            return (
                nt(dquery, query_weight[...])
                + nt(dkey, key_weight[...])
                + nt(dvalue, value_weight[...])
                + nn(dlatent, down[...])
            )

        def rest(value):
            cotangent[r, :] = dfirst[r, :] + value
            sent.append(copies.start(cotangent.at[r, :], grad_out.at[r, :]))

        return products, rest

    run_tasks(
        [
            project_task(
                tokens, lambda: low, query_weight, query_rows, setter(queries), head_scale, waits[1].wait
            ),
            project_task(tokens, None, key_weight, None, setter(keys), None, dense_copies),
            project_task(tokens, lambda: low, value_weight, value_rows, setter(values)),
            *short_attention_tasks(queries, keys, values, bias, context, shares, rows),
            *dense_tasks(
                tokens, context, dense, gains, hidden, out, kept, dict(out=dense_waits, written=write_out)
            ),
            *short_attention_back_tasks(
                queries, keys, values, dcontext, shares, dqueries, dkeys, dvalues, rows
            ),
            finish(slice(0, rows // 2)),
            finish(slice(rows // 2, rows)),
        ]
    )
    dquery, dvalue = dqueries[...], dvalues[...].astype(bf16)
    up_out[0:RANK, :] = adapter_scale * tn(low, dquery)[0:RANK, :]
    up_out[RANK : 2 * RANK, :] = adapter_scale * tn(low, dvalue)[RANK : 2 * RANK, :]
    for copy in sent:
        copy.wait()


def long_kernel(
    lengths_in, factors_in, attention_gain_in, output_gain_in, short_up_in,
    tokens_in, far_in, cotangent_in, query_in, key_in, value_in, out_in, inner_in, outer_in,
    out_out, near_out, far_out, up_out,
    tokens, far, cotangent, query_weight, key_weight, value_weight, out_weight, inner_weight, outer_weight,
    down, query_rows, value_rows, queries, keys, values, context, shares,
    unit, inverse, dfirst, slope, hidden, out, dlow, low, lengths, gain, gain_out, short_up, semaphores,
):
    rows, width = tokens.shape
    items = lengths.shape[0]
    half = rows // items
    copies = Copies(semaphores)
    small = start_all(
        copies,
        (
            *factor_pairs(factors_in, (down, query_rows, value_rows)), (lengths_in, lengths),
            (attention_gain_in, gain), (output_gain_in, gain_out), (short_up_in, short_up),
        ),
    )
    waits = start_all(
        copies,
        (
            (tokens_in, tokens), (query_in, query_weight), (far_in, far), (key_in, key_weight),
            (value_in, value_weight),
        ),
    )
    clear_tails((down, query_rows, value_rows))
    place = lax.axis_index("blk")

    def part(item, which):
        start = 2 * item * half + (place if which == 0 else 1 - place) * half
        return pl.ds(pl.multiple_of(start, half), half)

    def put(target, which, value):
        for item in range(items):
            target[part(item, which), :] = value[item * half : (item + 1) * half]

    for wait in small:
        wait.wait()
    gains = (gain[...].reshape(1, width), gain_out[...].reshape(1, width))
    waits[0].wait()
    low[0:rows, :] = nt(tokens[...], down[...]).astype(bf16)
    waits[1].wait()
    queries[...] = project_to(tokens[...], low[0:rows, :], query_weight[...], query_rows[...], head_scale)
    for wait in waits[2:5]:
        wait.wait()
    waits += start_all(
        copies,
        (
            (out_in, out_weight), (inner_in, inner_weight), (outer_in, outer_weight), (cotangent_in, cotangent),
        ),
    )
    low[rows:, :] = nt(far[...], down[...]).astype(bf16)
    put(keys, 0, project_to(tokens[...], None, key_weight[...], None))
    put(keys, 1, project_to(far[...], None, key_weight[...], None))
    put(values, 0, project_to(tokens[...], low[0:rows, :], value_weight[...], value_rows[...]))
    put(values, 1, project_to(far[...], low[rows:, :], value_weight[...], value_rows[...]))

    units = [
        (
            item * GROUPS + index, item, slice(index * WIDE, (index + 1) * WIDE),
            slice(item * half, (item + 1) * half), slice(2 * item * half, 2 * (item + 1) * half),
        )
        for item in range(items)
        for index in range(GROUPS)
    ]
    place_in_half = lax.broadcasted_iota(jnp.int32, (half, LANES), 0) + half
    masks = []
    for item in range(items):
        mask = jnp.where(place_in_half < lengths[item], 0.0, masked_score)
        masks.append(jnp.concatenate([mask] * (STACK * half // LANES), axis=1))

    def forward(number, item, columns, own, joined):
        def products():
            return nt(keys[joined, columns], stack_heads(queries[own, columns]))

        def rest(scores):
            scores = jnp.concatenate([scores[0:half], scores[half:] + masks[item]], axis=0)
            exact = softmax_columns(scores).astype(bf16)
            shares[number] = exact
            turned = jnp.swapaxes(values[joined, columns], 0, 1)
            context[own, columns] = join_heads(turned, exact, half).astype(bf16)

        return products, rest

    run_tasks([forward(*unit_) for unit_ in units])
    for wait in waits[5:]:
        wait.wait()
    dense = (out_weight, inner_weight, outer_weight)
    dcontext = context
    kept = dict(
        unit=unit, inverse=inverse, dfirst=dfirst, slope=slope, dlow=dlow, cotangent=cotangent, dcontext=dcontext,
    )
    run_tasks(dense_tasks(tokens, context, dense, gains, hidden, out, kept))
    sent = [copies.start(out, out_out)]
    dqueries = dlow
    dkeys = hidden.at[:, 0 : 2 * width]
    dvalues = hidden.at[:, 2 * width : 4 * width]

    def backward(number, item, columns, own, joined):
        def products():
            dstacked = stack_heads(dcontext[own, columns])
            return dstacked, nt(values[joined, columns], dstacked)

        def rest(value):
            dstacked, dshares = value
            exact = shares[number].astype(f32)
            inner = jnp.sum(exact * dshares, axis=0, keepdims=True)
            dscores = (exact * (dshares - inner)).astype(bf16)
            turned = jnp.swapaxes(keys[joined, columns], 0, 1)
            dqueries[own, columns] = (join_heads(turned, dscores, half) * head_scale).astype(bf16)
            dkey = nn(dscores, stack_heads(queries[own, columns])).astype(bf16)
            dvalue = nn(shares[number], dstacked).astype(bf16)
            for which in range(2):
                rows_ = slice(which * half, (which + 1) * half)
                target = slice(which * width + columns.start, which * width + columns.stop)
                dkeys[own, target] = dkey[rows_]
                dvalues[own, target] = dvalue[rows_]

        return products, rest

    run_tasks([backward(*unit_) for unit_ in units])

    def back_part(which):
        start = pl.multiple_of((place if which == 0 else 1 - place) * width, LANES)
        return dkeys[:, pl.ds(start, width)], dvalues[:, pl.ds(start, width)]

    dkey, dvalue = back_part(1)
    dlatent = nt(dvalue, value_rows[...]).astype(bf16)
    unit[...] = nt(dkey, key_weight[...]) + nt(dvalue, value_weight[...]) + nn(dlatent, down[...])
    sent.append(copies.start(unit, far_out))
    up = tn(low[rows:, :], dvalue)[RANK : 2 * RANK, :]
    dquery = dqueries[...]
    dkey, dvalue = back_part(0)
    dlatent = (nt(dquery, query_rows[...]) + nt(dvalue, value_rows[...])).astype(bf16)
    for r in (slice(0, rows // 2), slice(rows // 2, rows)):
        cotangent[r, :] = (
            dfirst[r, :]
            + nt(dquery[r], query_weight[...])
            + nt(dkey[r], key_weight[...])
            + nt(dvalue[r], value_weight[...])
            + nn(dlatent[r], down[...])
        )
        sent.append(copies.start(cotangent.at[r, :], near_out.at[r, :]))
    up = up + tn(low[0:rows, :], dvalue)[RANK : 2 * RANK, :]
    up_out[0:RANK, :] = adapter_scale * tn(low[0:rows, :], dquery)[0:RANK, :] + short_up[0:RANK, :]
    up_out[RANK : 2 * RANK, :] = adapter_scale * up + short_up[RANK : 2 * RANK, :]
    for copy in sent:
        copy.wait()


def eval_attention_kernel(
    lengths_in, factors_in, after,
    tokens_in, query_in, key_in, value_in,
    context,
    tokens, query_weight, key_weight, value_weight,
    down, query_rows, value_rows, bias, queries, keys, values, lengths, semaphores,
):
    rows, width = tokens.shape
    copies = Copies(semaphores)
    small = start_all(
        copies, ((lengths_in, lengths), *factor_pairs(factors_in, (down, query_rows, value_rows)))
    )
    waits = start_all(
        copies,
        (
            (tokens_in, tokens), (key_in, key_weight), (query_in, query_weight), (value_in, value_weight),
        ),
    )
    clear_tails((down, query_rows, value_rows))
    for wait in small:
        wait.wait()
    segment_bias(lengths, bias, rows)
    waits[0].wait()

    def merged(weight, extra):
        return lambda: (weight[...].astype(f32) + tn(down[...], extra[...])).astype(bf16)

    run_tasks(
        [
            project_task(tokens, None, key_weight, None, setter(keys), None, waits[1].wait),
            project_task(
                tokens, None, merged(query_weight, query_rows), None, setter(queries), head_scale, waits[2].wait
            ),
            project_task(
                tokens, None, merged(value_weight, value_rows), None, setter(values), None, waits[3].wait
            ),
            *short_attention_tasks(queries, keys, values, bias, context, None, rows),
        ]
    )


def eval_dense_kernel(
    attention_gain_in, output_gain_in, after,
    tokens_in, context_in, out_in, inner_in, outer_in, near_in, far_in,
    out_out, grad_out,
    tokens, context, out_weight, inner_weight, outer_weight, near, far, unit, hidden, gain, gain_out, semaphores,
):
    width = tokens.shape[1]
    copies = Copies(semaphores)
    first = start_all(
        copies,
        (
            (attention_gain_in, gain), (output_gain_in, gain_out),
            (context_in, context), (out_in, out_weight), (tokens_in, tokens),
        ),
    )
    inner = {}
    for start in range(0, hidden.shape[1], CHUNK):
        columns = slice(start, start + CHUNK)
        inner[start] = copies.start(inner_in.at[:, columns], inner_weight.at[:, columns])
    outer, *last = start_all(copies, ((outer_in, outer_weight), (near_in, near), (far_in, far)))
    ready = {("inner", start): copy.wait for start, copy in inner.items()}
    ready["outer"] = outer.wait
    ready["unit"] = unit
    for wait in first:
        wait.wait()
    gains = (gain[...].reshape(1, width), gain_out[...].reshape(1, width))
    dense = (out_weight, inner_weight, outer_weight)
    tasks = dense_tasks(tokens, context, dense, gains, hidden, out_out, None, ready)
    sent = []

    def gradient_waits():
        for wait in last:
            wait.wait()

    def gradient_sum(unused):
        near[...] = near[...] + far[...]
        sent.append(copies.start(near, grad_out))

    tasks.insert(len(tasks) - 4, (gradient_waits, gradient_sum))
    run_tasks(tasks)
    sent[0].wait()


IN_VMEM = pl.BlockSpec(memory_space=pltpu.VMEM)
IN_SMEM = pl.BlockSpec(memory_space=pltpu.SMEM)
ANYWHERE = pl.BlockSpec(memory_space=pl.ANY)
FACTORS = [IN_VMEM] * 4


def kernel_call(kernel, in_specs, out_specs, out_shape, scratch, copies, flops, moved, name):
    return pl.pallas_call(
        kernel,
        in_specs=in_specs,
        out_specs=out_specs,
        out_shape=out_shape,
        scratch_shapes=[*scratch, pltpu.SemaphoreType.DMA((copies,))],
        compiler_params=pltpu.CompilerParams(vmem_limit_bytes=VMEM_LIMIT),
        cost_estimate=pl.CostEstimate(flops=int(flops), bytes_accessed=int(moved), transcendentals=0),
        name=name,
    )


def shape(dims, kind):
    return jax.ShapeDtypeStruct(dims, kind)


def vm(dims, kind):
    return pltpu.VMEM(dims, kind)


def weight_room(width, wide):
    square = vm((width, width), bf16)
    return [square, square, square, square, vm((width, wide), bf16), vm((wide, width), bf16)]


def factor_room(width):
    return [vm((LANES, width), bf16)] * 3


def kept_room(rows, width, wide):
    return [
        vm((rows, width), f32), vm((rows, 1), f32), vm((rows, width), f32),
        vm((rows, wide), f32), vm((rows, wide), bf16), vm((rows, width), bf16), vm((rows, width), bf16),
    ]


def partner(value, axis, mask):
    count = lax.axis_size(axis)
    return lax.ppermute(value, axis, [(i, i ^ mask) for i in range(count)])


def quad_parts(value, axis, bit):
    masks = [mask * bit for mask in (1, 2, 3) if mask * bit < lax.axis_size(axis)]
    return [value, *[partner(value, axis, mask) for mask in masks]]


def add_up(parts):
    return functools.reduce(lambda a, b: a + b, parts)


def run_short(lengths, factors, gains, tokens, cotangent, weights):
    rows, width = tokens.shape
    wide = weights[4].shape[1]
    blocks = rows // BLOCK
    return kernel_call(
        short_kernel,
        [IN_SMEM, *FACTORS, IN_VMEM, IN_VMEM, *[ANYWHERE] * 8],
        [ANYWHERE, ANYWHERE, IN_VMEM, ANYWHERE],
        [
            shape((rows, width), bf16), shape((rows, width), f32), shape((2 * RANK, width), f32),
            shape((6 * RANK, width), bf16),
        ],
        [
            vm((rows, width), bf16), vm((rows, width), f32), *weight_room(width, wide), *factor_room(width),
            vm((blocks, WINDOW, BLOCK), f32), *[vm((rows, width), bf16)] * 4,
            vm((GROUPS, blocks, WINDOW, STACK * BLOCK), f32), *kept_room(rows, width, wide),
        ],
        16, 20e9, 25e6, "short_step",
    )(lengths, *factors, *gains, tokens, cotangent, *weights)


def run_long(lengths, factors, gains, short_up, tokens, far, cotangent, weights):
    rows, width = tokens.shape
    wide = weights[4].shape[1]
    items = lengths.shape[0]
    half = rows // items
    return kernel_call(
        long_kernel,
        [ANYWHERE] * 14,
        [ANYWHERE, ANYWHERE, ANYWHERE, IN_VMEM],
        [
            shape((rows, width), bf16), shape((rows, width), f32), shape((rows, width), f32),
            shape((2 * RANK, width), f32),
        ],
        [
            vm((rows, width), bf16), vm((rows, width), bf16), vm((rows, width), f32),
            *weight_room(width, wide), *factor_room(width), vm((rows, width), bf16),
            *[vm((2 * rows, width), bf16)] * 2, vm((rows, width), bf16),
            vm((items * GROUPS, 2 * half, STACK * half), bf16), *kept_room(rows, width, wide),
            vm((2 * rows, LANES), bf16), pltpu.SMEM((items,), jnp.int32), vm((width,), f32), vm((width,), f32),
            vm((2 * RANK, width), f32),
        ],
        24, 22e9, 30e6, "long_step",
    )(lengths, factors, *gains, short_up, tokens, far, cotangent, *weights)


def run_eval_attention(lengths, factors, after, tokens, weights):
    rows, width = tokens.shape
    blocks = rows // BLOCK
    return kernel_call(
        eval_attention_kernel,
        [ANYWHERE] * 7,
        IN_VMEM,
        shape((rows, width), bf16),
        [
            vm((rows, width), bf16), *[vm((width, width), bf16)] * 3, *factor_room(width),
            vm((blocks, WINDOW, BLOCK), f32), *[vm((rows, width), bf16)] * 3,
            pltpu.SMEM(lengths.shape, jnp.int32),
        ],
        8, 4e9, 6e6, "eval_attention",
    )(lengths, factors, after, tokens, *weights[0:3])


def run_eval_dense(gains, after, tokens, context, weights, near, far):
    rows, width = tokens.shape
    wide = weights[4].shape[1]
    return kernel_call(
        eval_dense_kernel,
        [ANYWHERE] * 10,
        [IN_VMEM, ANYWHERE],
        [shape((rows, width), bf16), shape((rows, width), f32)],
        [
            vm((rows, width), bf16), vm((rows, width), bf16), *weight_room(width, wide)[3:],
            vm((rows, width), f32), vm((rows, width), f32), vm((rows, width), f32), vm((rows, wide), bf16),
            vm((width,), f32), vm((width,), f32),
        ],
        12, 6e9, 18e6, "eval_dense",
    )(*gains, after, tokens, context, *weights[3:], near, far)


def body(
    short_tokens, short_lengths, long_tokens, long_lengths, eval_tokens, eval_lengths,
    query_matrix, key_weight, value_matrix, out_weight, inner_weight, outer_weight,
    query_down_factor, query_up_factor, value_down_factor, value_up_factor,
    attention_gain, output_gain, cot_short, cot_long,
):
    items, half, width = long_tokens.shape
    factors = (query_down_factor.T, query_up_factor, value_down_factor.T, value_up_factor)
    gains = (attention_gain, output_gain)
    weights = (query_matrix, key_weight, value_matrix, out_weight, inner_weight, outer_weight)

    long_flat = long_tokens.reshape(items * half, width)
    far_flat = partner(long_flat, "blk", 1)
    short_out, short_grad, short_up, packed = run_short(
        short_lengths, factors, gains, short_tokens, cot_short, weights
    )
    long_out, near_grad, far_grad, up = run_long(
        long_lengths, packed, gains, short_up, long_flat, far_flat,
        cot_long.reshape(items * half, width), weights,
    )
    up = up + partner(up, "blk", 1)
    up, far_grad = lax.optimization_barrier((up, far_grad))
    arrived = partner(far_grad, "blk", 1)

    stages = []
    bit = 1
    while bit < lax.axis_size("dp"):
        stages.append(bit)
        bit *= 4
    parts = quad_parts(up, "dp", stages[0])
    context = run_eval_attention(eval_lengths, packed, up, eval_tokens, weights)
    context, arrived, *parts = lax.optimization_barrier((context, arrived, *parts))
    first_sum = add_up(parts)
    for bit in stages[1:]:
        parts = quad_parts(add_up(parts), "dp", bit)
    eval_out, long_grad = run_eval_dense(
        gains, first_sum, eval_tokens, context, weights, near_grad, arrived
    )
    eval_out, *parts = lax.optimization_barrier((eval_out, *parts))
    query_up_grad = add_up([part[0:RANK] for part in parts])
    value_up_grad = add_up([part[RANK:] for part in parts])

    return (
        short_out,
        long_out.reshape(items, half, width),
        short_grad,
        long_grad.reshape(items, half, width),
        query_up_grad,
        value_up_grad,
        eval_out,
    )


def solution(mesh):
    rows = P(("dp", "blk"), None)
    items = P("dp", "blk", None)
    return jax.shard_map(
        body,
        mesh=mesh,
        in_specs=(
            rows, rows, items, P("dp"), rows, rows, *[P()] * 12, rows, items,
        ),
        out_specs=(rows, items, rows, items, P(), P(), rows),
        check_vma=False,
    )
```
